128 devices in a mesh: row: 8 (over z, core), col: 16 (over y, x).
Axes of the slice: x: 4, y: 4, z: 4, core: 2. Of those that a mesh axis runs over, the one named last changes fastest.
Arguments:
- trailing: float32 [20480, 20480], P('row', 'col'), may hold values from -24 to 24
- panel_block: float32 [20480, 128], P(('row', 'col')), may hold values from -0.2795085 to 0.2795085
Outputs:
- trailing_out: float32 [20480, 20480], P('row', 'col')
- r_factor: float32 [128, 128], replicated
- first_factor: float32 [128, 128], replicated
The draws below stay inside these ranges and needn't reach their ends.
All inputs are finite; a program needn't handle non-finite values.
Results may differ from the reference program's by a relative error of at most 0.0003.
Values sent between devices are 32-bit elements; how exact they have to be, the bound alone decides.
A program may use at most 128 MiB of HBM per device.

```python
import math
import jax
import jax.numpy as jnp
from jax import lax

M = 20480
NB = 128


def draw_trailing(key, part):
    noise = jnp.clip(jax.random.normal(key, (M, M), jnp.float32), -6.0, 6.0)
    symmetric = 0.5 * (noise + noise.T)
    return jnp.clip(symmetric, -24.0, 24.0)


def draw_panel_block(key, part):
    spreads = jnp.exp(jax.random.uniform(jax.random.fold_in(key, 3), (NB,), jnp.float32, math.log(0.03), math.log(0.3)))
    rising = 1.0 + 4.0 * jnp.arange(M, dtype=jnp.float32) / (M - 1.0)
    shared = jnp.clip(jax.random.normal(jax.random.fold_in(key, 5), (M,), jnp.float32), -4.0, 4.0)
    private = jnp.clip(jax.random.normal(key, (M, NB), jnp.float32), -4.0, 4.0)
    row_scales = rising
    values = (shared[:, None] + spreads[None, :] * private) * row_scales[:, None] * M ** (-0.5)
    bound = 40.0 * M ** (-0.5)
    return jnp.clip(values, -bound, bound)


def setup_inputs(seed: int = 0) -> dict:
    streams_of = jax.random.split(jax.random.key(seed), 3)
    trailing = draw_trailing(jax.random.fold_in(streams_of[2], 71), 0)
    panel_block = draw_panel_block(jax.random.fold_in(streams_of[2], 71), 0)
    return {"trailing": trailing, "panel_block": panel_block}


HIGHEST = lax.Precision.HIGHEST

def gram_of(block):
    return jnp.dot(block.T.astype(jnp.float32), block.astype(jnp.float32), preferred_element_type=jnp.float32, precision=HIGHEST)

def reference(trailing, panel_block):
    low_one = jnp.linalg.cholesky(gram_of(panel_block))
    first_q = lax.linalg.triangular_solve(low_one, panel_block, left_side=False, lower=True, transpose_a=True)
    low_two = jnp.linalg.cholesky(gram_of(first_q))
    ortho_basis = lax.linalg.triangular_solve(low_two, first_q, left_side=False, lower=True, transpose_a=True)
    r_factor = jnp.dot(low_two.T.astype(jnp.float32), low_one.T.astype(jnp.float32), preferred_element_type=jnp.float32, precision=HIGHEST)
    products = jnp.dot(trailing.astype(jnp.float32), ortho_basis.astype(jnp.float32), preferred_element_type=jnp.float32, precision=HIGHEST)
    projected = jnp.dot(ortho_basis.T.astype(jnp.float32), products.astype(jnp.float32), preferred_element_type=jnp.float32, precision=HIGHEST)
    correction = 2.0 * (products - jnp.dot(ortho_basis.astype(jnp.float32), projected.astype(jnp.float32), preferred_element_type=jnp.float32, precision=HIGHEST))
    left_factor = jnp.concatenate([ortho_basis, correction], axis=1)
    right_factor = jnp.concatenate([correction, ortho_basis], axis=1)
    trailing_out = trailing - jnp.dot(left_factor.astype(jnp.float32), right_factor.T.astype(jnp.float32), preferred_element_type=jnp.float32, precision=HIGHEST)
    return (trailing_out, r_factor, low_one.T)
```

```python
import jax
import jax.numpy as jnp
from jax import lax
from jax.experimental import pallas as pl
from jax.experimental.pallas import tpu as pltpu
from jax.sharding import PartitionSpec as P

HIGHEST = lax.Precision.HIGHEST
MESH = pl.DeviceIdType.MESH
F32 = jnp.float32
BF16 = jnp.bfloat16

ROWS = 8
COLS = 16
NB = 128
SHARD = 160
ROW_BLOCK = SHARD * COLS
COL_BLOCK = SHARD * ROWS


def dot(first, second, contract, precision=HIGHEST):
    return lax.dot_general(
        first, second, (contract, ((), ())), precision=precision, preferred_element_type=F32
    )


def split(value):
    high = value.astype(BF16)
    return high, (value - high.astype(F32)).astype(BF16)


def factor(work, gram, step=32):
    down = lax.broadcasted_iota(jnp.int32, (NB, NB), 0)
    across = lax.broadcasted_iota(jnp.int32, (NB, NB), 1)
    work[:, :NB] = gram
    work[:, NB:] = jnp.where(down == across, 1.0, 0.0)
    sub = lax.broadcasted_iota(jnp.int32, (step, 1), 0)
    for base in range(0, NB, step):
        rows = work[base : base + step, :]
        tall = [
            jnp.broadcast_to(rows[:, base + k : base + k + 1], (step, NB)) for k in range(step)
        ]
        for k in range(step):
            scale = lax.rsqrt(tall[k][k : k + 1, :])
            low = tall[k] * scale
            for m in range(k + 1, step):
                tall[m] = tall[m] - low * low[m : m + 1, :]
            top = rows[k : k + 1, :] * jnp.concatenate([scale, scale], axis=1)
            low = jnp.where(sub > k, low, 0.0)
            rows = jnp.where(sub == k, top, rows - jnp.concatenate([low, low], axis=1) * top)
        work[base : base + step, :] = rows
        if base + step < NB:
            change = dot(rows[:, :NB], rows, ((0,), (0,)))
            work[base + step :, :] = work[base + step :, :] - change[base + step :, :]
    work[:, :NB] = jnp.where(across >= down, work[:, :NB], 0.0)
    work[:, NB:] = jnp.where(across <= down, work[:, NB:], 0.0)


class Exchange:
    def __init__(self, size, me, place, source, target, send_sem, recv_sem):
        self.size, self.me, self.place = size, me, place
        self.source, self.target = source, target
        self.send_sem, self.recv_sem = send_sem, recv_sem

    def each(self, action):
        def body(step, carry):
            action(lax.rem(self.me + step, self.size))
            return carry

        lax.fori_loop(1, self.size, body, 0)

    def copy(self, peer, slot):
        row, col = self.place(peer)
        return pltpu.make_async_remote_copy(
            src_ref=self.source(peer),
            dst_ref=self.target(slot),
            send_sem=self.send_sem.at[peer],
            recv_sem=self.recv_sem.at[slot],
            device_id=(row, col),
            device_id_type=MESH,
        )

    def start(self):
        self.each(lambda peer: self.copy(peer, self.me).start())

    def receive(self):
        self.each(lambda peer: self.copy(peer, peer).wait_recv())

    def finish(self):
        self.each(lambda peer: self.copy(peer, peer).wait_send())


def blocks(ref, size):
    return lambda index: ref.at[pl.ds(pl.multiple_of(index * size, size), size), :]


def panel_kernel(
    trailing_hbm, panel,
    left_x, left_y, right, r_out, first_out,
    a_full, a_high, a_low, p_rows, q_rows, q_wide, p_cols, q_cols,
    y_part, y_buf, y_cols, y_rows,
    g_own, g_buf, g_part, g_all, h_own, h_buf, h_part, h_all,
    work_one, work_two,
    a_sem, send16, recv16, send8, recv8, perm_send, perm_recv,
):
    me_r, me_c = lax.axis_index("row"), lax.axis_index("col")
    in_row = lambda peer: (me_r, peer)
    in_col = lambda peer: (peer, me_c)
    to_cols = (lax.rem(me_c, 8), 2 * me_r + me_c // 8)
    to_rows = (me_c // 2, 8 * lax.rem(me_c, 2) + me_r)
    fixed = jnp.logical_and(to_cols[0] == me_r, to_cols[1] == me_c)

    load = pltpu.make_async_copy(trailing_hbm, a_full, a_sem)
    load.start()

    barrier = pltpu.get_barrier_semaphore()

    def greet(size, me, place):
        def body(step, carry):
            pl.semaphore_signal(
                barrier, inc=1, device_id=place(lax.rem(me + step, size)), device_id_type=MESH
            )
            return carry

        lax.fori_loop(1, size, body, 0)

    greet(COLS, me_c, in_row)
    greet(ROWS, me_r, in_col)

    @pl.when(jnp.logical_not(fixed))
    def _():
        pl.semaphore_signal(barrier, inc=1, device_id=to_cols, device_id_type=MESH)
        pl.semaphore_signal(barrier, inc=1, device_id=to_rows, device_id_type=MESH)

    g_own[...] = dot(panel[...], panel[...], ((0,), (0,)))
    my_rows = pl.ds(pl.multiple_of(me_r * SHARD, SHARD), SHARD)
    my_cols = pl.ds(pl.multiple_of(me_c * SHARD, SHARD), SHARD)
    p_rows[my_cols, :] = panel[...]

    pl.semaphore_wait(barrier, jnp.where(fixed, COLS + ROWS - 2, COLS + ROWS))

    def permute(source, target, place, slot, sem):
        return pltpu.make_async_remote_copy(
            src_ref=source, dst_ref=blocks(target, SHARD)(slot),
            send_sem=perm_send.at[sem], recv_sem=perm_recv.at[sem],
            device_id=place, device_id_type=MESH,
        )

    def total(buf, own, count):
        value = own
        for k in range(count):
            part = buf[k * 8 : k * 8 + 8, :]
            value = part if k == 0 else value + part
        return value

    eight = lambda index: pl.ds(pl.multiple_of(index * 8, 8), 8)

    def summed(own, buf, part, full, sem):
        scatter = Exchange(
            COLS, me_c, in_row, blocks(own, 8), blocks(buf, 8), send16.at[sem], recv16.at[sem]
        )
        share = Exchange(
            ROWS, me_r, in_col, lambda peer: blocks(part, 8)(me_r), blocks(part, 8),
            send8.at[sem], recv8.at[sem],
        )
        gather = Exchange(
            COLS, me_c, in_row, lambda peer: blocks(full, 8)(me_c), blocks(full, 8),
            send16.at[sem + 1], recv16.at[sem + 1],
        )

        def one():
            buf[eight(me_c), :] = own[eight(me_c), :]
            scatter.start()

        def two():
            scatter.receive()
            part[eight(me_r), :] = total(buf, None, COLS)
            share.start()

        def three():
            share.receive()
            full[eight(me_c), :] = total(part, None, ROWS)
            gather.start()

        def four():
            gather.receive()

        def finish():
            scatter.finish()
            share.finish()
            gather.finish()

        return one, two, three, four, finish

    one, two, three, four, gram_finish = summed(g_own, g_buf, g_part, g_all, 0)
    one()

    @pl.when(jnp.logical_not(fixed))
    def _():
        permute(panel, p_cols, to_cols, to_cols[0], 0).start()

    @pl.when(fixed)
    def _():
        p_cols[my_rows, :] = panel[...]

    two()

    @pl.when(jnp.logical_not(fixed))
    def _():
        permute(panel, p_cols, to_cols, me_r, 0).wait_recv()

    three()
    panel_rows = Exchange(
        COLS, me_c, in_row, lambda peer: panel, blocks(p_rows, SHARD), send16.at[4], recv16.at[4]
    )
    panel_rows.start()
    panel_cols = Exchange(
        ROWS, me_r, in_col, lambda peer: blocks(p_cols, SHARD)(me_r), blocks(p_cols, SHARD),
        send8.at[4], recv8.at[4],
    )
    panel_cols.start()
    load.wait()

    def split_rows(index, carry):
        rows = pl.ds(pl.multiple_of(index * 64, 64), 64)
        a_high[rows, :], a_low[rows, :] = split(a_full[rows, :])
        return carry

    lax.fori_loop(0, ROW_BLOCK // 64, split_rows, 0)
    four()
    factor(work_one, g_all[...])
    first_out[...] = work_one[:, :NB]
    inverse = work_one[:, NB:]

    panel_rows.receive()

    def basis_rows(index, carry):
        rows = pl.ds(pl.multiple_of(index * 256, 256), 256)
        value = dot(p_rows[rows, :], inverse, ((1,), (1,)))
        q_rows[rows, :] = value
        high, low = split(value.T)
        q_wide[:NB, rows] = high
        q_wide[NB:, rows] = low
        return carry

    lax.fori_loop(0, ROW_BLOCK // 256, basis_rows, 0)
    panel_cols.receive()

    def basis_cols(index, carry):
        rows = pl.ds(pl.multiple_of(index * 256, 256), 256)
        q_cols[rows, :] = dot(p_cols[rows, :], inverse, ((1,), (1,)))
        return carry

    lax.fori_loop(0, COL_BLOCK // 256, basis_cols, 0)

    def products(index, carry):
        cols = pl.ds(pl.multiple_of(index * 256, 256), 256)
        wide = dot(q_wide[...], a_high[:, cols], ((1,), (0,)), None)
        value = wide[:NB, :] + wide[NB:, :] + dot(q_wide[:NB, :], a_low[:, cols], ((1,), (0,)), None)
        y_part[cols, :] = value.T
        return carry

    lax.fori_loop(0, COL_BLOCK // 256, products, 0)

    y_scatter = Exchange(
        ROWS, me_r, in_col, blocks(y_part, SHARD), blocks(y_buf, SHARD), send8.at[5], recv8.at[5]
    )
    y_scatter.start()
    y_buf[my_rows, :] = y_part[my_rows, :]
    mine = q_rows[my_cols, :]
    h_own[:, :NB] = dot(mine, mine, ((0,), (0,)))
    h_own[:, NB:] = dot(q_cols[...], y_part[...], ((0,), (0,)))
    one, two, three, four, more_finish = summed(h_own, h_buf, h_part, h_all, 2)
    one()
    y_scatter.receive()
    value = y_buf[:SHARD, :]
    for k in range(1, ROWS):
        value = value + y_buf[k * SHARD : (k + 1) * SHARD, :]
    y_cols[my_rows, :] = value
    y_shard = blocks(y_cols, SHARD)(me_r)

    @pl.when(jnp.logical_not(fixed))
    def _():
        permute(y_shard, y_rows, to_rows, to_rows[1], 1).start()

    @pl.when(fixed)
    def _():
        y_rows[my_cols, :] = y_cols[my_rows, :]

    y_columns = Exchange(
        ROWS, me_r, in_col, lambda peer: y_shard, blocks(y_cols, SHARD), send8.at[6], recv8.at[6]
    )
    y_columns.start()
    two()

    @pl.when(jnp.logical_not(fixed))
    def _():
        permute(y_shard, y_rows, to_rows, me_c, 1).wait_recv()

    three()
    y_gather = Exchange(
        COLS, me_c, in_row, lambda peer: blocks(y_rows, SHARD)(me_c), blocks(y_rows, SHARD),
        send16.at[5], recv16.at[5],
    )
    y_gather.start()
    four()

    factor(work_two, h_all[:, :NB])
    r_out[...] = dot(work_two[:, :NB], work_one[:, :NB], ((1,), (0,)))
    second = work_two[:, NB:]
    gram_inverse = dot(second, second, ((0,), (0,)))
    core = 4.0 * h_all[:, NB:]

    def finish_x(index, carry):
        rows = pl.ds(pl.multiple_of(index * 256, 256), 256)
        left_x[rows, :] = dot(q_rows[rows, :], gram_inverse, ((1,), (0,)))
        return carry

    lax.fori_loop(0, ROW_BLOCK // 256, finish_x, 0)
    y_columns.receive()

    def finish_right(index, carry):
        rows = pl.ds(pl.multiple_of(index * 256, 256), 256)
        x_tile = dot(q_cols[rows, :], gram_inverse, ((1,), (0,)))
        right[rows, :NB] = 2.0 * y_cols[rows, :] - dot(x_tile, core, ((1,), (0,)))
        right[rows, NB:] = 2.0 * x_tile
        return carry

    lax.fori_loop(0, COL_BLOCK // 256, finish_right, 0)
    y_gather.receive()
    left_y[...] = y_rows[...]

    gram_finish()
    panel_rows.finish()
    panel_cols.finish()
    y_scatter.finish()
    more_finish()
    y_columns.finish()
    y_gather.finish()

    @pl.when(jnp.logical_not(fixed))
    def _():
        permute(panel, p_cols, to_cols, to_cols[0], 0).wait_send()
        permute(y_shard, y_rows, to_rows, to_rows[1], 1).wait_send()


def panel_call(trailing, panel_block):
    vmem = pl.BlockSpec(memory_space=pltpu.VMEM)
    shape = lambda *dims: jax.ShapeDtypeStruct(dims, F32)
    tall, wide = (ROW_BLOCK, NB), (COL_BLOCK, NB)
    f32 = lambda *dims: pltpu.VMEM(dims, F32)
    bf16 = lambda *dims: pltpu.VMEM(dims, BF16)
    dma = lambda *dims: pltpu.SemaphoreType.DMA(dims)
    return pl.pallas_call(
        panel_kernel,
        out_shape=[
            shape(*tall), shape(*tall), shape(COL_BLOCK, 2 * NB), shape(NB, NB), shape(NB, NB)
        ],
        in_specs=[pl.BlockSpec(memory_space=pl.ANY), vmem],
        out_specs=[vmem] * 5,
        scratch_shapes=[
            f32(ROW_BLOCK, COL_BLOCK), bf16(ROW_BLOCK, COL_BLOCK), bf16(ROW_BLOCK, COL_BLOCK),
            f32(*tall), f32(*tall), bf16(2 * NB, ROW_BLOCK), f32(*wide), f32(*wide),
            f32(*wide), f32(*wide), f32(*wide), f32(*tall),
            f32(NB, NB), f32(NB, NB), f32(8 * ROWS, NB), f32(NB, NB),
            f32(NB, 2 * NB), f32(NB, 2 * NB), f32(8 * ROWS, 2 * NB), f32(NB, 2 * NB),
            f32(NB, 2 * NB), f32(NB, 2 * NB),
            pltpu.SemaphoreType.DMA, dma(6, COLS), dma(6, COLS), dma(7, ROWS), dma(7, ROWS),
            dma(2), dma(2),
        ],
        compiler_params=pltpu.CompilerParams(
            collective_id=0, has_side_effects=True, vmem_limit_bytes=56 * 1024 * 1024
        ),
        name="panel",
    )(trailing, panel_block)


def on_device(trailing, panel_block):
    left_x, left_y, right, r_factor, first_factor = panel_call(trailing, panel_block)
    left = jnp.concatenate([left_x, left_y], axis=1)
    change = jnp.dot(left, right.T, preferred_element_type=F32, precision=lax.Precision.HIGH)
    return trailing - change, r_factor, first_factor


def solution(mesh):
    in_specs = (P("row", "col"), P(("row", "col"), None))
    out_specs = (P("row", "col"), P(), P())
    return jax.shard_map(
        on_device, mesh=mesh, in_specs=in_specs, out_specs=out_specs, check_vma=False
    )
```

```python
import jax
import jax.numpy as jnp
from jax import lax
from jax.experimental import pallas as pl
from jax.experimental.pallas import tpu as pltpu
from jax.sharding import PartitionSpec as P

HIGHEST = lax.Precision.HIGHEST
MESH = pl.DeviceIdType.MESH
F32 = jnp.float32
BF16 = jnp.bfloat16

ROWS = 8
COLS = 16
SIDE = 4
NB = 128
SHARD = 160
HALF = 80
ROW_BLOCK = SHARD * COLS
COL_BLOCK = SHARD * ROWS
TILE = 256


def dot(first, second, contract, precision=HIGHEST):
    return lax.dot_general(
        first, second, (contract, ((), ())), precision=precision, preferred_element_type=F32
    )


def split(value):
    high = value.astype(BF16)
    return high, (value - high.astype(F32)).astype(BF16)


def factor(work, gram, step=32):
    down = lax.broadcasted_iota(jnp.int32, (NB, NB), 0)
    across = lax.broadcasted_iota(jnp.int32, (NB, NB), 1)
    work[:, :NB] = gram
    work[:, NB:] = jnp.where(down == across, 1.0, 0.0)
    sub = lax.broadcasted_iota(jnp.int32, (step, 1), 0)
    for base in range(0, NB, step):
        rows = work[base : base + step, :]
        tall = [
            jnp.broadcast_to(rows[:, base + k : base + k + 1], (step, NB)) for k in range(step)
        ]
        for k in range(step):
            scale = lax.rsqrt(tall[k][k : k + 1, :])
            low = tall[k] * scale
            for m in range(k + 1, step):
                tall[m] = tall[m] - low * low[m : m + 1, :]
            top = rows[k : k + 1, :] * jnp.concatenate([scale, scale], axis=1)
            low = jnp.where(sub > k, low, 0.0)
            rows = jnp.where(sub == k, top, rows - jnp.concatenate([low, low], axis=1) * top)
        work[base : base + step, :] = rows
        if base + step < NB:
            change = dot(rows[:, :NB], rows, ((0,), (0,)))
            work[base + step :, :] = work[base + step :, :] - change[base + step :, :]
    work[:, :NB] = jnp.where(across >= down, work[:, :NB], 0.0)
    work[:, NB:] = jnp.where(across <= down, work[:, NB:], 0.0)


class Exchange:
    def __init__(self, size, me, place, source, target, send_sem, recv_sem):
        self.size, self.me, self.place = size, me, place
        self.source, self.target = source, target
        self.send_sem, self.recv_sem = send_sem, recv_sem

    def each(self, action):
        def body(step, carry):
            action(lax.rem(self.me + step, self.size))
            return carry

        lax.fori_loop(1, self.size, body, 0)

    def copy(self, peer, slot):
        return pltpu.make_async_remote_copy(
            src_ref=self.source(peer),
            dst_ref=self.target(slot),
            send_sem=self.send_sem.at[peer],
            recv_sem=self.recv_sem.at[slot],
            device_id=self.place(peer),
            device_id_type=MESH,
        )

    def start(self):
        self.each(lambda peer: self.copy(peer, self.me).start())

    def receive(self):
        self.each(lambda peer: self.copy(peer, peer).wait_recv())

    def finish(self):
        self.each(lambda peer: self.copy(peer, peer).wait_send())


class Swap:
    def __init__(self, apart, place, source, target, there, here, send_sem, recv_sem):
        self.apart, self.here, self.source, self.target = apart, here, source, target
        self.copy = lambda slot: pltpu.make_async_remote_copy(
            src_ref=source, dst_ref=target(slot), send_sem=send_sem, recv_sem=recv_sem,
            device_id=place, device_id_type=MESH,
        )
        self.there = there

    def start(self):
        @pl.when(self.apart)
        def _():
            self.copy(self.there).start()

        @pl.when(jnp.logical_not(self.apart))
        def _():
            self.target(self.here)[...] = self.source[...]

    def receive(self):
        @pl.when(self.apart)
        def _():
            self.copy(self.here).wait_recv()

    def finish(self):
        @pl.when(self.apart)
        def _():
            self.copy(self.there).wait_send()


def eights(ref):
    return lambda index: ref.at[pl.ds(pl.multiple_of(index * 8, 8), 8), :]


def panel_kernel(
    trailing_hbm, panel,
    left_high, left_low, right_high, right_low, r_out, first_out,
    a_full, a_high, a_low, p_rows, q_rows, q_wide, p_cols, q_cols,
    y_part, y_mate, y_half, y_ring, y_cols, y_rows,
    g_own, g_buf, g_part, g_all, h_own, h_buf, h_part, h_all,
    work_one, work_two,
    a_sem, plane_send, plane_recv, axis_send, axis_recv, ring_send, ring_recv, one_send, one_recv,
):
    me_r, me_c = lax.axis_index("row"), lax.axis_index("col")
    z, core = me_r // 2, lax.rem(me_r, 2)
    y, x = me_c // SIDE, lax.rem(me_c, SIDE)
    in_plane = lambda peer: (me_r, peer)
    in_axis = lambda peer: (peer, me_c)
    in_x = lambda peer: (me_r, y * SIDE + peer)
    in_y = lambda peer: (me_r, peer * SIDE + x)
    in_z = lambda peer: (2 * peer + core, me_c)
    mate = (2 * z + 1 - core, me_c)
    out_r, out_c = lax.rem(me_c, ROWS), 2 * me_r + me_c // ROWS
    in_r, in_c = me_c // 2, ROWS * lax.rem(me_c, 2) + me_r
    apart = jnp.logical_not(jnp.logical_and(out_r == me_r, out_c == me_c))
    straight = core == x // 2
    turn_r = 2 * y + jnp.where(straight, core, 1 - core)
    turn_c = z * SIDE + jnp.where(straight, x, SIDE - 1 - x)
    turned = jnp.logical_not(jnp.logical_and(straight, y == z))

    load = pltpu.make_async_copy(trailing_hbm, a_full, a_sem)
    load.start()

    barrier = pltpu.get_barrier_semaphore()

    def signal(place):
        pl.semaphore_signal(barrier, inc=1, device_id=place, device_id_type=MESH)

    def greet(size, me, place):
        def body(step, carry):
            signal(place(lax.rem(me + step, size)))
            return carry

        lax.fori_loop(1, size, body, 0)

    greet(COLS, me_c, in_plane)
    greet(ROWS, me_r, in_axis)

    @pl.when(apart)
    def _():
        signal((out_r, out_c))
        signal((in_r, in_c))

    @pl.when(turned)
    def _():
        signal((turn_r, turn_c))

    g_own[...] = dot(panel[...], panel[...], ((0,), (0,)))
    for half in range(2):
        p_rows[y, x, half] = panel[half * HALF : (half + 1) * HALF, :]
    pl.semaphore_wait(
        barrier, COLS + ROWS - 2 + jnp.where(apart, 2, 0) + jnp.where(turned, 1, 0)
    )

    def summed(own, buf, part, full, sem):
        scatter = Exchange(
            COLS, me_c, in_plane, eights(own), eights(buf),
            plane_send.at[sem], plane_recv.at[sem],
        )
        share = Exchange(
            ROWS, me_r, in_axis, lambda peer: eights(part)(me_r), eights(part),
            axis_send.at[sem], axis_recv.at[sem],
        )
        gather = Exchange(
            COLS, me_c, in_plane, lambda peer: eights(full)(me_c), eights(full),
            plane_send.at[sem + 2], plane_recv.at[sem + 2],
        )

        def total(source, count):
            value = source[:8, :]
            for k in range(1, count):
                value = value + source[k * 8 : k * 8 + 8, :]
            return value

        def one():
            eights(buf)(me_c)[...] = eights(own)(me_c)[...]
            scatter.start()

        def two():
            scatter.receive()
            eights(part)(me_r)[...] = total(buf, COLS)
            share.start()

        def three():
            share.receive()
            eights(full)(me_c)[...] = total(part, ROWS)
            gather.start()

        def finish():
            scatter.finish()
            share.finish()
            gather.finish()

        return one, two, three, gather.receive, finish

    def ring(place, me, source, target, sem):
        return Exchange(SIDE, me, place, source, target, ring_send.at[sem], ring_recv.at[sem])

    def plane_gather(rows, sem):
        first = (
            ring(in_y, y, lambda peer: rows.at[y, x, 0], lambda slot: rows.at[slot, x, 0], sem),
            ring(in_x, x, lambda peer: rows.at[y, x, 1], lambda slot: rows.at[y, slot, 1], sem + 1),
        )
        second = (
            ring(in_x, x, lambda peer: rows.at[:, x, 0], lambda slot: rows.at[:, slot, 0], sem + 2),
            ring(in_y, y, lambda peer: rows.at[y, :, 1], lambda slot: rows.at[slot, :, 1], sem + 3),
        )
        return first, second

    def start(pair):
        for item in pair:
            item.start()

    def receive(pair):
        for item in pair:
            item.receive()

    def axis_gather(cols, sem, mate_sem):
        along = ring(
            in_z, z, lambda peer: cols.at[z, core], lambda slot: cols.at[slot, core], sem
        )
        across = Swap(
            True, mate, cols.at[:, core], lambda slot: cols.at[:, slot], core, 1 - core,
            one_send.at[mate_sem], one_recv.at[mate_sem],
        )
        return along, across

    one, two, three, gram_all, gram_finish = summed(g_own, g_buf, g_part, g_all, 0)
    p_first, p_second = plane_gather(p_rows, 0)
    p_swap = Swap(
        apart, (out_r, out_c), panel, lambda slot: p_cols.at[slot // 2, lax.rem(slot, 2)],
        out_r, me_r, one_send.at[0], one_recv.at[0],
    )
    p_along, p_across = axis_gather(p_cols, 8, 1)
    one()
    start(p_first)
    two()
    p_swap.start()
    three()
    receive(p_first)
    start(p_second)
    load.wait()

    def split_rows(index, carry):
        rows = pl.ds(pl.multiple_of(index * 64, 64), 64)
        a_high[rows, :], a_low[rows, :] = split(a_full[rows, :])
        return carry

    lax.fori_loop(0, ROW_BLOCK // 64, split_rows, 0)
    gram_all()
    p_swap.receive()
    p_along.start()
    factor(work_one, g_all[...])
    first_out[...] = work_one[:, :NB]
    inverse = work_one[:, NB:]
    p_along.receive()
    p_across.start()
    receive(p_second)

    def basis_rows(index, carry):
        wide = SIDE * SHARD
        rows = pl.ds(pl.multiple_of(index * wide, wide), wide)
        value = dot(p_rows[index].reshape(wide, NB), inverse, ((1,), (1,)))
        q_rows[rows, :] = value
        high, low = split(value.T)
        q_wide[:NB, rows] = high
        q_wide[NB:, rows] = low
        return carry

    lax.fori_loop(0, SIDE, basis_rows, 0)

    def products(index, carry):
        cols = pl.ds(pl.multiple_of(index * TILE, TILE), TILE)
        wide = dot(q_wide[...], a_high[:, cols], ((1,), (0,)), None)
        value = wide[:NB, :] + wide[NB:, :]
        value = value + dot(q_wide[:NB, :], a_low[:, cols], ((1,), (0,)), None)
        y_part[cols, :] = value.T
        return carry

    lax.fori_loop(0, COL_BLOCK // TILE, products, 0)

    piece = lambda place, k: pl.ds(pl.multiple_of((2 * place + k) * SHARD, SHARD), SHARD)
    y_pair = [
        pltpu.make_async_remote_copy(
            src_ref=y_part.at[piece(k, 1 - core), :], dst_ref=y_mate.at[k],
            send_sem=one_send.at[4 + k], recv_sem=one_recv.at[4 + k],
            device_id=mate, device_id_type=MESH,
        )
        for k in range(SIDE)
    ]
    for item in y_pair:
        item.start()

    def basis_cols(index, carry):
        rows = pl.ds(pl.multiple_of(index * 2 * SHARD, 2 * SHARD), 2 * SHARD)
        q_cols[rows, :] = dot(p_cols[index].reshape(2 * SHARD, NB), inverse, ((1,), (1,)))
        return carry

    for k in range(SIDE):
        y_pair[k].wait_recv()
        y_half[k] = y_part[piece(k, core), :] + y_mate[k]
    y_along = ring(in_z, z, lambda peer: y_half.at[peer], lambda slot: y_ring.at[slot], 9)
    y_along.start()
    p_across.receive()
    lax.fori_loop(0, SIDE, basis_cols, 0)
    mine = q_rows[pl.ds(pl.multiple_of(me_c * SHARD, SHARD), SHARD), :]
    h_own[:, :NB] = dot(mine, mine, ((0,), (0,)))
    h_own[:, NB:] = dot(q_cols[...], y_part[...], ((0,), (0,)))
    one, two, three, more_all, more_finish = summed(h_own, h_buf, h_part, h_all, 1)
    one()
    y_ring[z] = y_half[z]
    y_along.receive()
    y_cols[z, core] = y_ring[0] + y_ring[1] + (y_ring[2] + y_ring[3])
    y_first, y_second = plane_gather(y_rows, 4)
    y_swaps = [
        Swap(
            turned, (turn_r, turn_c), y_cols.at[z, core, pl.ds(half * HALF, HALF)],
            lambda slot, half=half: y_rows.at[slot // SIDE, lax.rem(slot, SIDE), half],
            turn_c, me_c, one_send.at[2 + half], one_recv.at[2 + half],
        )
        for half in range(2)
    ]
    y_columns, y_across = axis_gather(y_cols, 10, 8)
    start(y_swaps)
    two()
    y_columns.start()
    receive(y_swaps)
    start(y_first)
    three()
    receive(y_first)
    start(y_second)
    y_columns.receive()
    y_across.start()
    more_all()

    factor(work_two, h_all[:, :NB])
    r_out[...] = dot(work_two[:, :NB], work_one[:, :NB], ((1,), (0,)))
    second = work_two[:, NB:]
    gram_inverse = dot(second, second, ((0,), (0,)))
    center = 4.0 * h_all[:, NB:]

    def finish_x(index, carry):
        rows = pl.ds(pl.multiple_of(index * TILE, TILE), TILE)
        high, low = split(dot(q_rows[rows, :], gram_inverse, ((1,), (0,))))
        left_high[rows, :NB] = high
        left_low[rows, :NB] = low
        return carry

    lax.fori_loop(0, ROW_BLOCK // TILE, finish_x, 0)
    y_across.receive()

    def finish_right(index, carry):
        rows = pl.ds(pl.multiple_of(index * 2 * SHARD, 2 * SHARD), 2 * SHARD)
        x_tile = dot(q_cols[rows, :], gram_inverse, ((1,), (0,)))
        mixed = 2.0 * y_cols[index].reshape(2 * SHARD, NB) - dot(x_tile, center, ((1,), (0,)))
        right_high[rows, :NB], right_low[rows, :NB] = split(mixed)
        right_high[rows, NB:], right_low[rows, NB:] = split(2.0 * x_tile)
        return carry

    lax.fori_loop(0, SIDE, finish_right, 0)
    receive(y_second)

    def finish_y(index, carry):
        down, over = index // SIDE, lax.rem(index, SIDE)
        same = over // 2 == core
        source_x = jnp.where(same, over, SIDE - 1 - over)
        source_core = jnp.where(same, core, 1 - core)
        rank = lax.rem(source_x, 2) * ROWS + 2 * down + source_core
        rows = pl.ds(pl.multiple_of(rank * SHARD, SHARD), SHARD)
        left_high[rows, NB:], left_low[rows, NB:] = split(y_rows[down, over].reshape(SHARD, NB))
        return carry

    lax.fori_loop(0, COLS, finish_y, 0)

    gram_finish()
    more_finish()
    for item in (*p_first, *p_second, p_swap, p_along, p_across, y_along):
        item.finish()
    for item in (*y_swaps, *y_first, *y_second, y_columns, y_across):
        item.finish()
    for item in y_pair:
        item.wait_send()


def panel_call(trailing, panel_block):
    vmem = pl.BlockSpec(memory_space=pltpu.VMEM)
    f32 = lambda *dims: pltpu.VMEM(dims, F32)
    bf16 = lambda *dims: pltpu.VMEM(dims, BF16)
    dma = lambda *dims: pltpu.SemaphoreType.DMA(dims)
    left = jax.ShapeDtypeStruct((ROW_BLOCK, 2 * NB), BF16)
    right = jax.ShapeDtypeStruct((COL_BLOCK, 2 * NB), BF16)
    small = jax.ShapeDtypeStruct((NB, NB), F32)
    plane = f32(SIDE, SIDE, 2, HALF, NB)
    axis = f32(SIDE, 2, SHARD, NB)
    ring = f32(SIDE, SHARD, NB)
    return pl.pallas_call(
        panel_kernel,
        out_shape=[left, left, right, right, small, small],
        in_specs=[pl.BlockSpec(memory_space=pl.ANY), vmem],
        out_specs=[vmem] * 6,
        scratch_shapes=[
            f32(ROW_BLOCK, COL_BLOCK), bf16(ROW_BLOCK, COL_BLOCK), bf16(ROW_BLOCK, COL_BLOCK),
            plane, f32(ROW_BLOCK, NB), bf16(2 * NB, ROW_BLOCK), axis, f32(COL_BLOCK, NB),
            f32(COL_BLOCK, NB), ring, ring, ring, axis, plane,
            f32(NB, NB), f32(NB, NB), f32(8 * ROWS, NB), f32(NB, NB),
            f32(NB, 2 * NB), f32(NB, 2 * NB), f32(8 * ROWS, 2 * NB), f32(NB, 2 * NB),
            f32(NB, 2 * NB), f32(NB, 2 * NB),
            pltpu.SemaphoreType.DMA, dma(4, COLS), dma(4, COLS), dma(2, ROWS), dma(2, ROWS),
            dma(11, SIDE), dma(11, SIDE), dma(9), dma(9),
        ],
        compiler_params=pltpu.CompilerParams(
            collective_id=0, has_side_effects=True, vmem_limit_bytes=56 * 1024 * 1024
        ),
        name="panel",
    )(trailing, panel_block)


def update_kernel(
    trailing, left_high, left_low, right_high, right_low, r_in, first_in, out, r_out, first_out
):
    change = dot(left_high[...], right_high[...], ((1,), (1,)), None)
    change = change + dot(left_high[...], right_low[...], ((1,), (1,)), None)
    change = change + dot(left_low[...], right_high[...], ((1,), (1,)), None)
    out[...] = trailing[...] - change

    @pl.when(pl.program_id(0) == 0)
    def _():
        r_out[...] = r_in[...]
        first_out[...] = first_in[...]


def update_call(trailing, left_high, left_low, right_high, right_low, r_factor, first_factor):
    tile = pl.BlockSpec((TILE, COL_BLOCK), lambda i: (i, 0))
    left = pl.BlockSpec((TILE, 2 * NB), lambda i: (i, 0))
    right = pl.BlockSpec((COL_BLOCK, 2 * NB), lambda i: (0, 0))
    small = pl.BlockSpec((NB, NB), lambda i: (0, 0))
    return pl.pallas_call(
        update_kernel,
        grid=(ROW_BLOCK // TILE,),
        out_shape=[
            jax.ShapeDtypeStruct((ROW_BLOCK, COL_BLOCK), F32),
            jax.ShapeDtypeStruct((NB, NB), F32),
            jax.ShapeDtypeStruct((NB, NB), F32),
        ],
        in_specs=[tile, left, left, right, right, small, small],
        out_specs=[tile, small, small],
        compiler_params=pltpu.CompilerParams(
            dimension_semantics=("arbitrary",), vmem_limit_bytes=40 * 1024 * 1024
        ),
        name="update",
    )(trailing, left_high, left_low, right_high, right_low, r_factor, first_factor)


def on_device(trailing, panel_block):
    pieces = panel_call(trailing, panel_block)
    return tuple(update_call(trailing, *pieces))


def solution(mesh):
    in_specs = (P("row", "col"), P(("row", "col"), None))
    out_specs = (P("row", "col"), P(), P())
    return jax.shard_map(
        on_device, mesh=mesh, in_specs=in_specs, out_specs=out_specs, check_vma=False
    )
```

```python
import jax
import jax.numpy as jnp
from jax import lax
from jax.experimental import pallas as pl
from jax.experimental.pallas import tpu as pltpu
from jax.sharding import PartitionSpec as P

HIGHEST = lax.Precision.HIGHEST
MESH = pl.DeviceIdType.MESH
F32 = jnp.float32
BF16 = jnp.bfloat16

ROWS = 8
COLS = 16
SIDE = 4
NB = 128
SHARD = 160
HALF = 80
ROW_BLOCK = SHARD * COLS
COL_BLOCK = SHARD * ROWS
TILE = 256
STEP = 32
SLOTS = 3
WIDE = SIDE * SHARD


def dot(first, second, contract, precision=HIGHEST):
    return lax.dot_general(
        first, second, (contract, ((), ())), precision=precision, preferred_element_type=F32
    )


def split(value):
    high = value.astype(BF16)
    return high, (value - high.astype(F32)).astype(BF16)


def factor(work, gram=None, bases=range(0, NB, STEP)):
    step = STEP
    down = lax.broadcasted_iota(jnp.int32, (NB, NB), 0)
    across = lax.broadcasted_iota(jnp.int32, (NB, NB), 1)
    if gram is not None:
        work[:, :NB] = gram
        work[:, NB:] = jnp.where(down == across, 1.0, 0.0)
    sub = lax.broadcasted_iota(jnp.int32, (step, 1), 0)
    for base in bases:
        rows = work[base : base + step, :]
        tall = [
            jnp.broadcast_to(rows[:, base + k : base + k + 1], (step, NB)) for k in range(step)
        ]
        for k in range(step):
            scale = lax.rsqrt(tall[k][k : k + 1, :])
            low = tall[k] * scale
            for m in range(k + 1, step):
                tall[m] = tall[m] - low * low[m : m + 1, :]
            top = rows[k : k + 1, :] * jnp.concatenate([scale, scale], axis=1)
            low = jnp.where(sub > k, low, 0.0)
            rows = jnp.where(sub == k, top, rows - jnp.concatenate([low, low], axis=1) * top)
        work[base : base + step, :] = rows
        if base + step < NB:
            change = dot(rows[:, :NB], rows, ((0,), (0,)))
            work[base + step :, :] = work[base + step :, :] - change[base + step :, :]
    if bases[-1] == NB - step:
        work[:, :NB] = jnp.where(across >= down, work[:, :NB], 0.0)
        work[:, NB:] = jnp.where(across <= down, work[:, NB:], 0.0)


class Exchange:
    def __init__(self, size, me, place, source, target, send_sem, recv_sem):
        self.size, self.me, self.place = size, me, place
        self.source, self.target = source, target
        self.send_sem, self.recv_sem = send_sem, recv_sem

    def each(self, action):
        def body(step, carry):
            action(lax.rem(self.me + step, self.size))
            return carry

        lax.fori_loop(1, self.size, body, 0)

    def copy(self, peer, slot):
        return pltpu.make_async_remote_copy(
            src_ref=self.source(peer),
            dst_ref=self.target(slot),
            send_sem=self.send_sem.at[peer],
            recv_sem=self.recv_sem.at[slot],
            device_id=self.place(peer),
            device_id_type=MESH,
        )

    def start(self):
        self.each(lambda peer: self.copy(peer, self.me).start())

    def receive(self):
        self.each(lambda peer: self.copy(peer, peer).wait_recv())

    def finish(self):
        self.each(lambda peer: self.copy(peer, peer).wait_send())


class Swap:
    def __init__(self, apart, place, source, target, there, here, send_sem, recv_sem):
        self.apart, self.here, self.source, self.target = apart, here, source, target
        self.copy = lambda slot: pltpu.make_async_remote_copy(
            src_ref=source, dst_ref=target(slot), send_sem=send_sem, recv_sem=recv_sem,
            device_id=place, device_id_type=MESH,
        )
        self.there = there

    def start(self):
        @pl.when(self.apart)
        def _():
            self.copy(self.there).start()

        @pl.when(jnp.logical_not(self.apart))
        def _():
            self.target(self.here)[...] = self.source[...]

    def receive(self):
        @pl.when(self.apart)
        def _():
            self.copy(self.here).wait_recv()

    def finish(self):
        @pl.when(self.apart)
        def _():
            self.copy(self.there).wait_send()


def eights(ref):
    return lambda index: ref.at[pl.ds(pl.multiple_of(index * 8, 8), 8), :]


def panel_kernel(
    trailing_hbm, panel,
    a_full, left_high, left_low, right, r_out, first_out,
    a_high, a_low, p_rows, q_rows, q_wide, p_cols, q_cols,
    y_part, y_mate, y_half, y_ring, y_cols, y_rows,
    g_own, g_buf, g_part, g_all, h_own, h_buf, h_part, h_all, s_own, s_buf, s_part, s_all,
    work_one, work_two,
    a_sem, plane_send, plane_recv, axis_send, axis_recv, ring_send, ring_recv, one_send, one_recv,
):
    me_r, me_c = lax.axis_index("row"), lax.axis_index("col")
    z, core = me_r // 2, lax.rem(me_r, 2)
    y, x = me_c // SIDE, lax.rem(me_c, SIDE)
    in_plane = lambda peer: (me_r, peer)
    in_axis = lambda peer: (peer, me_c)
    in_x = lambda peer: (me_r, y * SIDE + peer)
    in_y = lambda peer: (me_r, peer * SIDE + x)
    in_z = lambda peer: (2 * peer + core, me_c)
    mate = (2 * z + 1 - core, me_c)
    out_r, out_c = lax.rem(me_c, ROWS), 2 * me_r + me_c // ROWS
    in_r, in_c = me_c // 2, ROWS * lax.rem(me_c, 2) + me_r
    apart = jnp.logical_not(jnp.logical_and(out_r == me_r, out_c == me_c))
    straight = core == x // 2
    turn_r = 2 * y + jnp.where(straight, core, 1 - core)
    turn_c = z * SIDE + jnp.where(straight, x, SIDE - 1 - x)
    turned = jnp.logical_not(jnp.logical_and(straight, y == z))

    load = pltpu.make_async_copy(trailing_hbm, a_full, a_sem)
    load.start()
    barrier = pltpu.get_barrier_semaphore()

    def signal(place):
        pl.semaphore_signal(barrier, inc=1, device_id=place, device_id_type=MESH)

    def greet(size, me, place):
        def body(step, carry):
            signal(place(lax.rem(me + step, size)))
            return carry

        lax.fori_loop(1, size, body, 0)

    greet(COLS, me_c, in_plane)
    greet(ROWS, me_r, in_axis)

    @pl.when(apart)
    def _():
        signal((out_r, out_c))
        signal((in_r, in_c))

    @pl.when(turned)
    def _():
        signal((turn_r, turn_c))

    g_own[...] = dot(panel[...], panel[...], ((0,), (0,)))
    for half in range(2):
        p_rows[y, x, half] = panel[half * HALF : (half + 1) * HALF, :]
    pl.semaphore_wait(
        barrier, COLS + ROWS - 2 + jnp.where(apart, 2, 0) + jnp.where(turned, 1, 0)
    )

    def summed(own, buf, part, full, sem):
        scatter = Exchange(
            COLS, me_c, in_plane, eights(own), eights(buf),
            plane_send.at[sem], plane_recv.at[sem],
        )
        share = Exchange(
            ROWS, me_r, in_axis, lambda peer: eights(part)(me_r), eights(part),
            axis_send.at[sem], axis_recv.at[sem],
        )
        gather = Exchange(
            COLS, me_c, in_plane, lambda peer: eights(full)(me_c), eights(full),
            plane_send.at[sem + 3], plane_recv.at[sem + 3],
        )

        def total(source, count):
            value = source[:8, :]
            for k in range(1, count):
                value = value + source[k * 8 : k * 8 + 8, :]
            return value

        def one():
            eights(buf)(me_c)[...] = eights(own)(me_c)[...]
            scatter.start()

        def two():
            scatter.receive()
            eights(part)(me_r)[...] = total(buf, COLS)
            share.start()

        def three():
            share.receive()
            eights(full)(me_c)[...] = total(part, ROWS)
            gather.start()

        def finish():
            scatter.finish()
            share.finish()
            gather.finish()

        return one, two, three, gather.receive, finish

    def ring(place, me, source, target, sem):
        return Exchange(SIDE, me, place, source, target, ring_send.at[sem], ring_recv.at[sem])

    def plane_gather(rows, sem):
        first = (
            ring(in_y, y, lambda peer: rows.at[y, x, 0], lambda slot: rows.at[slot, x, 0], sem),
            ring(in_x, x, lambda peer: rows.at[y, x, 1], lambda slot: rows.at[y, slot, 1], sem + 1),
        )
        second = (
            ring(in_x, x, lambda peer: rows.at[:, x, 0], lambda slot: rows.at[:, slot, 0], sem + 2),
            ring(in_y, y, lambda peer: rows.at[y, :, 1], lambda slot: rows.at[slot, :, 1], sem + 3),
        )
        return first, second

    def start(pair):
        for item in pair:
            item.start()

    def receive(pair):
        for item in pair:
            item.receive()

    def axis_gather(cols, sem, mate_sem):
        along = ring(
            in_z, z, lambda peer: cols.at[z, core], lambda slot: cols.at[slot, core], sem
        )
        across = Swap(
            True, mate, cols.at[:, core], lambda slot: cols.at[:, slot], core, 1 - core,
            one_send.at[mate_sem], one_recv.at[mate_sem],
        )
        return along, across

    one, two, three, gram_all, gram_finish = summed(g_own, g_buf, g_part, g_all, 0)
    p_first, p_second = plane_gather(p_rows, 0)
    p_swap = Swap(
        apart, (out_r, out_c), panel, lambda slot: p_cols.at[slot // 2, lax.rem(slot, 2)],
        out_r, me_r, one_send.at[0], one_recv.at[0],
    )
    p_along, p_across = axis_gather(p_cols, 8, 1)
    one()
    start(p_first)
    two()
    p_swap.start()
    three()
    receive(p_first)
    start(p_second)
    load.wait()

    def split_rows(index, carry):
        rows = pl.ds(pl.multiple_of(index * 64, 64), 64)
        a_high[rows, :], a_low[rows, :] = split(a_full[rows, :])
        return carry

    lax.fori_loop(0, ROW_BLOCK // 64, split_rows, 0)
    gram_all()
    p_swap.receive()
    p_along.start()
    factor(work_one, g_all[...])
    first_out[...] = work_one[:, :NB]
    inverse = work_one[:, NB:]
    p_along.receive()
    p_across.start()
    receive(p_second)

    def basis_rows(index, carry):
        rows = pl.ds(pl.multiple_of(index * WIDE, WIDE), WIDE)
        value = dot(p_rows[index].reshape(WIDE, NB), inverse, ((1,), (1,)))
        q_rows[rows, :] = value
        high, low = split(value.T)
        q_wide[:NB, rows] = high
        q_wide[NB:, rows] = low
        return carry

    lax.fori_loop(0, SIDE, basis_rows, 0)
    mine = q_rows[pl.ds(pl.multiple_of(me_c * SHARD, SHARD), SHARD), :]
    h_own[...] = dot(mine, mine, ((0,), (0,)))
    one, two, three, more_all, more_finish = summed(h_own, h_buf, h_part, h_all, 1)
    one()

    piece = lambda place, k: pl.ds(pl.multiple_of((2 * place + k) * SHARD, SHARD), SHARD)
    y_pair = [
        pltpu.make_async_remote_copy(
            src_ref=y_part.at[piece(k, 1 - core), :], dst_ref=y_mate.at[k],
            send_sem=one_send.at[4 + k], recv_sem=one_recv.at[4 + k],
            device_id=mate, device_id_type=MESH,
        )
        for k in range(SIDE)
    ]

    def products(index, carry):
        cols = pl.ds(pl.multiple_of(index * TILE // 2, TILE // 2), TILE // 2)
        wide = dot(q_wide[...], a_high[:, cols], ((1,), (0,)), None)
        value = wide[:NB, :] + wide[NB:, :]
        value = value + dot(q_wide[:NB, :], a_low[:, cols], ((1,), (0,)), None)
        y_part[cols, :] = value.T
        return carry

    for half in range(2):
        lax.fori_loop(5 * half, 5 * half + 5, products, 0)
        y_pair[2 * half].start()
        y_pair[2 * half + 1].start()
    two()

    def basis_cols(index, carry):
        rows = pl.ds(pl.multiple_of(index * 2 * SHARD, 2 * SHARD), 2 * SHARD)
        q_cols[rows, :] = dot(p_cols[index].reshape(2 * SHARD, NB), inverse, ((1,), (1,)))
        return carry

    for k in range(SIDE):
        y_pair[k].wait_recv()
        y_half[k] = y_part[piece(k, core), :] + y_mate[k]
    y_along = ring(in_z, z, lambda peer: y_half.at[peer], lambda slot: y_ring.at[slot], 9)
    y_along.start()
    p_across.receive()
    lax.fori_loop(0, SIDE, basis_cols, 0)
    s_own[...] = dot(q_cols[...], y_part[...], ((0,), (0,)))
    center_one, center_two, center_three, center_all, center_finish = summed(
        s_own, s_buf, s_part, s_all, 2
    )
    center_one()
    three()
    y_ring[z] = y_half[z]
    y_along.receive()
    y_cols[z, core] = y_ring[0] + y_ring[1] + (y_ring[2] + y_ring[3])
    y_first, y_second = plane_gather(y_rows, 4)
    y_swaps = [
        Swap(
            turned, (turn_r, turn_c), y_cols.at[z, core, pl.ds(half * HALF, HALF)],
            lambda slot, half=half: y_rows.at[slot // SIDE, lax.rem(slot, SIDE), half],
            turn_c, me_c, one_send.at[2 + half], one_recv.at[2 + half],
        )
        for half in range(2)
    ]
    y_columns, y_across = axis_gather(y_cols, 10, 8)
    start(y_swaps)
    y_columns.start()
    center_two()
    more_all()
    factor(work_two, h_all[...], range(0, NB // 2, STEP))
    receive(y_swaps)
    start(y_first)
    factor(work_two, None, range(NB // 2, NB, STEP))
    center_three()
    receive(y_first)
    start(y_second)
    y_columns.receive()
    y_across.start()
    r_out[...] = dot(work_two[:, :NB], work_one[:, :NB], ((1,), (0,)))
    second = work_two[:, NB:]
    gram_inverse = dot(second, second, ((0,), (0,)))

    def finish_x(index, carry):
        rows = pl.ds(pl.multiple_of(index * TILE, TILE), TILE)
        high, low = split(dot(q_rows[rows, :], gram_inverse, ((1,), (0,))))
        left_high[rows, :NB] = high
        left_low[rows, :NB] = low
        return carry

    lax.fori_loop(0, ROW_BLOCK // TILE, finish_x, 0)
    center_all()
    center = 4.0 * s_all[...]
    y_across.receive()

    def finish_right(index, carry):
        rows = pl.ds(pl.multiple_of(index * WIDE, WIDE), WIDE)
        half = pl.ds(2 * index, 2)
        x_tile = dot(q_cols[rows, :], gram_inverse, ((1,), (0,)))
        mixed = 2.0 * y_cols[half].reshape(WIDE, NB) - dot(x_tile, center, ((1,), (0,)))
        for place, value in ((0, mixed), (NB, 2.0 * x_tile)):
            high, low = split(value.T)
            right[place : place + NB, rows] = high
            right[2 * NB + place : 3 * NB + place, rows] = low
            right[4 * NB + place : 5 * NB + place, rows] = high
        return carry

    lax.fori_loop(0, 2, finish_right, 0)
    receive(y_second)

    def finish_y(index, carry):
        down, over = index // SIDE, lax.rem(index, SIDE)
        same = over // 2 == core
        source_x = jnp.where(same, over, SIDE - 1 - over)
        source_core = jnp.where(same, core, 1 - core)
        rank = lax.rem(source_x, 2) * ROWS + 2 * down + source_core
        rows = pl.ds(pl.multiple_of(rank * SHARD, SHARD), SHARD)
        left_high[rows, NB:], left_low[rows, NB:] = split(y_rows[down, over].reshape(SHARD, NB))
        return carry

    lax.fori_loop(0, COLS, finish_y, 0)

    gram_finish()
    more_finish()
    center_finish()
    for item in (*p_first, *p_second, p_swap, p_along, p_across, y_along):
        item.finish()
    for item in (*y_swaps, *y_first, *y_second, y_columns, y_across):
        item.finish()
    for item in y_pair:
        item.wait_send()


def panel_call(trailing, panel_block):
    vmem = pl.BlockSpec(memory_space=pltpu.VMEM)
    f32 = lambda *dims: pltpu.VMEM(dims, F32)
    bf16 = lambda *dims: pltpu.VMEM(dims, BF16)
    dma = lambda *dims: pltpu.SemaphoreType.DMA(dims)
    left, small = bf16(ROW_BLOCK, 2 * NB), f32(NB, NB)
    plane = f32(SIDE, SIDE, 2, HALF, NB)
    axis = f32(SIDE, 2, SHARD, NB)
    ring = f32(SIDE, SHARD, NB)
    return pl.pallas_call(
        panel_kernel,
        out_shape=[f32(ROW_BLOCK, COL_BLOCK), left, left, bf16(6 * NB, COL_BLOCK), small, small],
        in_specs=[pl.BlockSpec(memory_space=pl.ANY), vmem],
        out_specs=[vmem] * 6,
        scratch_shapes=[
            bf16(ROW_BLOCK, COL_BLOCK), bf16(ROW_BLOCK, COL_BLOCK),
            plane, f32(ROW_BLOCK, NB), bf16(2 * NB, ROW_BLOCK), axis, f32(COL_BLOCK, NB),
            f32(COL_BLOCK, NB), ring, ring, ring, axis, plane,
            *(3 * [small, small, f32(8 * ROWS, NB), small]),
            f32(NB, 2 * NB), f32(NB, 2 * NB),
            pltpu.SemaphoreType.DMA, dma(6, COLS), dma(6, COLS), dma(3, ROWS), dma(3, ROWS),
            dma(11, SIDE), dma(11, SIDE), dma(9), dma(9),
        ],
        compiler_params=pltpu.CompilerParams(
            collective_id=0, has_side_effects=True, vmem_limit_bytes=36 * 1024 * 1024
        ),
        name="panel",
    )(trailing, panel_block)


def update_kernel(
    trailing, left_high, left_low, right, r_in, first_in, out, r_out, first_out, ready, sems
):
    def send(index, slot):
        rows = pl.ds(pl.multiple_of(index * TILE, TILE), TILE)
        return pltpu.make_async_copy(ready.at[slot], out.at[rows, :], sems.at[slot])

    def body(index, carry):
        slot = lax.rem(index, SLOTS)

        @pl.when(index >= SLOTS)
        def _():
            send(index - SLOTS, slot).wait()

        rows = pl.ds(pl.multiple_of(index * TILE, TILE), TILE)
        high = left_high[rows, :]
        left = jnp.concatenate([high, high, left_low[rows, :]], axis=1)
        ready[slot] = trailing[rows, :] - dot(left, right[...], ((1,), (0,)), None)
        send(index, slot).start()
        return carry

    count = ROW_BLOCK // TILE
    lax.fori_loop(0, count, body, 0)
    r_out[...] = r_in[...]
    first_out[...] = first_in[...]
    for index in range(count - SLOTS, count):
        send(index, index % SLOTS).wait()


def update_call(*pieces):
    vmem = pl.BlockSpec(memory_space=pltpu.VMEM)
    small = jax.ShapeDtypeStruct((NB, NB), F32)
    return pl.pallas_call(
        update_kernel,
        out_shape=[jax.ShapeDtypeStruct((ROW_BLOCK, COL_BLOCK), F32), small, small],
        in_specs=[vmem] * 6,
        out_specs=[pl.BlockSpec(memory_space=pltpu.HBM), vmem, vmem],
        scratch_shapes=[
            pltpu.VMEM((SLOTS, TILE, COL_BLOCK), F32), pltpu.SemaphoreType.DMA((SLOTS,))
        ],
        compiler_params=pltpu.CompilerParams(vmem_limit_bytes=8 * 1024 * 1024),
        name="update",
    )(*(pltpu.with_memory_space_constraint(piece, pltpu.VMEM) for piece in pieces))


def on_device(trailing, panel_block):
    pieces = panel_call(trailing, panel_block)
    return tuple(update_call(*pieces))


def solution(mesh):
    in_specs = (P("row", "col"), P(("row", "col"), None))
    out_specs = (P("row", "col"), P(), P())
    return jax.shard_map(
        on_device, mesh=mesh, in_specs=in_specs, out_specs=out_specs, check_vma=False
    )
```

```python
import jax
import jax.numpy as jnp
from jax import lax
from jax.experimental import pallas as pl
from jax.experimental.pallas import tpu as pltpu
from jax.sharding import PartitionSpec as P

HIGHEST = lax.Precision.HIGHEST
MESH = pl.DeviceIdType.MESH
F32 = jnp.float32
BF16 = jnp.bfloat16

ROWS = 8
COLS = 16
SIDE = 4
NB = 128
SHARD = 160
HALF = 80
ROW_BLOCK = SHARD * COLS
COL_BLOCK = SHARD * ROWS
TILE = 256
STEP = 32
SLOTS = 3
WIDE = SIDE * SHARD


def dot(first, second, contract, precision=HIGHEST):
    return lax.dot_general(
        first, second, (contract, ((), ())), precision=precision, preferred_element_type=F32
    )


def split(value):
    high = value.astype(BF16)
    return high, (value - high.astype(F32)).astype(BF16)


def dot3(first, second, contract):
    (a, b), (c, d) = split(first), split(second)
    value = dot(a, c, contract, None)
    return value + (dot(a, d, contract, None) + dot(b, c, contract, None))


def factor(work, gram=None, bases=range(0, NB, STEP)):
    step = STEP
    down = lax.broadcasted_iota(jnp.int32, (NB, NB), 0)
    across = lax.broadcasted_iota(jnp.int32, (NB, NB), 1)
    if gram is not None:
        work[:, :NB] = gram
        work[:, NB:] = jnp.where(down == across, 1.0, 0.0)
    sub = lax.broadcasted_iota(jnp.int32, (step, 1), 0)
    for base in bases:
        rows = work[base : base + step, :]
        tall = [
            jnp.broadcast_to(rows[:, base + k : base + k + 1], (step, NB)) for k in range(step)
        ]
        for k in range(step):
            scale = lax.rsqrt(tall[k][k : k + 1, :])
            low = tall[k] * scale
            for m in range(k + 1, step):
                tall[m] = tall[m] - low * low[m : m + 1, :]
            top = rows[k : k + 1, :] * jnp.concatenate([scale, scale], axis=1)
            low = jnp.where(sub > k, low, 0.0)
            rows = jnp.where(sub == k, top, rows - jnp.concatenate([low, low], axis=1) * top)
        work[base : base + step, :] = rows
        if base + step < NB:
            change = dot(rows[:, :NB], rows, ((0,), (0,)))
            work[base + step :, :] = work[base + step :, :] - change[base + step :, :]
    if bases[-1] == NB - step:
        work[:, :NB] = jnp.where(across >= down, work[:, :NB], 0.0)
        work[:, NB:] = jnp.where(across <= down, work[:, NB:], 0.0)


class Exchange:
    def __init__(self, size, me, place, source, target, send_sem, recv_sem):
        self.size, self.me, self.place = size, me, place
        self.source, self.target = source, target
        self.send_sem, self.recv_sem = send_sem, recv_sem

    def each(self, action):
        def body(step, carry):
            action(lax.rem(self.me + step, self.size))
            return carry

        lax.fori_loop(1, self.size, body, 0)

    def copy(self, peer, slot):
        return pltpu.make_async_remote_copy(
            src_ref=self.source(peer),
            dst_ref=self.target(slot),
            send_sem=self.send_sem.at[peer],
            recv_sem=self.recv_sem.at[slot],
            device_id=self.place(peer),
            device_id_type=MESH,
        )

    def start(self):
        self.each(lambda peer: self.copy(peer, self.me).start())

    def receive(self):
        self.each(lambda peer: self.copy(peer, peer).wait_recv())

    def finish(self):
        self.each(lambda peer: self.copy(peer, peer).wait_send())


class Swap:
    def __init__(self, apart, place, source, target, there, here, send_sem, recv_sem):
        self.apart, self.here, self.source, self.target = apart, here, source, target
        self.copy = lambda slot: pltpu.make_async_remote_copy(
            src_ref=source, dst_ref=target(slot), send_sem=send_sem, recv_sem=recv_sem,
            device_id=place, device_id_type=MESH,
        )
        self.there = there

    def start(self):
        @pl.when(self.apart)
        def _():
            self.copy(self.there).start()

        @pl.when(jnp.logical_not(self.apart))
        def _():
            self.target(self.here)[...] = self.source[...]

    def receive(self):
        @pl.when(self.apart)
        def _():
            self.copy(self.here).wait_recv()

    def finish(self):
        @pl.when(self.apart)
        def _():
            self.copy(self.there).wait_send()


def eights(ref):
    return lambda index: ref.at[pl.ds(pl.multiple_of(index * 8, 8), 8), :]


def panel_kernel(
    trailing_hbm, panel_hbm,
    a_full, left_high, left_low, right, r_out, first_out,
    panel, x_high, x_low, mixed_t, a_high, a_low, p_rows, q_rows, q_wide, p_cols, q_cols,
    y_part, y_mate, y_half, y_ring, y_cols, y_rows,
    g_own, g_buf, g_part, g_all, h_own, h_buf, h_part, h_all, s_own, s_buf, s_part, s_all,
    work_one, work_two,
    a_sem, panel_sem, plane_send, plane_recv, axis_send, axis_recv, ring_send, ring_recv, one_send, one_recv,
):
    me_r, me_c = lax.axis_index("row"), lax.axis_index("col")
    z, core = me_r // 2, lax.rem(me_r, 2)
    y, x = me_c // SIDE, lax.rem(me_c, SIDE)
    in_plane = lambda peer: (me_r, peer)
    in_axis = lambda peer: (peer, me_c)
    in_x = lambda peer: (me_r, y * SIDE + peer)
    in_y = lambda peer: (me_r, peer * SIDE + x)
    in_z = lambda peer: (2 * peer + core, me_c)
    mate = (2 * z + 1 - core, me_c)
    out_r, out_c = lax.rem(me_c, ROWS), 2 * me_r + me_c // ROWS
    in_r, in_c = me_c // 2, ROWS * lax.rem(me_c, 2) + me_r
    apart = jnp.logical_not(jnp.logical_and(out_r == me_r, out_c == me_c))
    straight = core == x // 2
    turn_r = 2 * y + jnp.where(straight, core, 1 - core)
    turn_c = z * SIDE + jnp.where(straight, x, SIDE - 1 - x)
    turned = jnp.logical_not(jnp.logical_and(straight, y == z))

    fetch = pltpu.make_async_copy(panel_hbm, panel, panel_sem)
    fetch.start()
    load = pltpu.make_async_copy(trailing_hbm, a_full, a_sem)
    load.start()
    barrier = pltpu.get_barrier_semaphore()

    def signal(place):
        pl.semaphore_signal(barrier, inc=1, device_id=place, device_id_type=MESH)

    def greet(size, me, place):
        def body(step, carry):
            signal(place(lax.rem(me + step, size)))
            return carry

        lax.fori_loop(1, size, body, 0)

    greet(COLS, me_c, in_plane)
    greet(ROWS, me_r, in_axis)

    @pl.when(apart)
    def _():
        signal((out_r, out_c))
        signal((in_r, in_c))

    @pl.when(turned)
    def _():
        signal((turn_r, turn_c))

    fetch.wait()
    g_own[...] = dot(panel[...], panel[...], ((0,), (0,)))
    for half in range(2):
        p_rows[y, x, half] = panel[half * HALF : (half + 1) * HALF, :]
    pl.semaphore_wait(
        barrier, COLS + ROWS - 2 + jnp.where(apart, 2, 0) + jnp.where(turned, 1, 0)
    )

    def summed(own, buf, part, full, sem):
        scatter = Exchange(
            COLS, me_c, in_plane, eights(own), eights(buf),
            plane_send.at[sem], plane_recv.at[sem],
        )
        share = Exchange(
            ROWS, me_r, in_axis, lambda peer: eights(part)(me_r), eights(part),
            axis_send.at[sem], axis_recv.at[sem],
        )
        gather = Exchange(
            COLS, me_c, in_plane, lambda peer: eights(full)(me_c), eights(full),
            plane_send.at[sem + 3], plane_recv.at[sem + 3],
        )

        def total(source, count):
            value = source[:8, :]
            for k in range(1, count):
                value = value + source[k * 8 : k * 8 + 8, :]
            return value

        def one():
            eights(buf)(me_c)[...] = eights(own)(me_c)[...]
            scatter.start()

        def two():
            scatter.receive()
            eights(part)(me_r)[...] = total(buf, COLS)
            share.start()

        def three():
            share.receive()
            eights(full)(me_c)[...] = total(part, ROWS)
            gather.start()

        def finish():
            scatter.finish()
            share.finish()
            gather.finish()

        return one, two, three, gather.receive, finish

    def ring(place, me, source, target, sem):
        return Exchange(SIDE, me, place, source, target, ring_send.at[sem], ring_recv.at[sem])

    def plane_gather(rows, sem):
        first = (
            ring(in_y, y, lambda peer: rows.at[y, x, 0], lambda slot: rows.at[slot, x, 0], sem),
            ring(in_x, x, lambda peer: rows.at[y, x, 1], lambda slot: rows.at[y, slot, 1], sem + 1),
        )
        second = (
            ring(in_x, x, lambda peer: rows.at[:, x, 0], lambda slot: rows.at[:, slot, 0], sem + 2),
            ring(in_y, y, lambda peer: rows.at[y, :, 1], lambda slot: rows.at[slot, :, 1], sem + 3),
        )
        return first, second

    def start(pair):
        for item in pair:
            item.start()

    def receive(pair):
        for item in pair:
            item.receive()

    def axis_gather(cols, sem, mate_sem):
        along = ring(
            in_z, z, lambda peer: cols.at[z, core], lambda slot: cols.at[slot, core], sem
        )
        across = Swap(
            True, mate, cols.at[:, core], lambda slot: cols.at[:, slot], core, 1 - core,
            one_send.at[mate_sem], one_recv.at[mate_sem],
        )
        return along, across

    one, two, three, gram_all, gram_finish = summed(g_own, g_buf, g_part, g_all, 0)
    p_first, p_second = plane_gather(p_rows, 0)
    p_swap = Swap(
        apart, (out_r, out_c), panel, lambda slot: p_cols.at[slot // 2, lax.rem(slot, 2)],
        out_r, me_r, one_send.at[0], one_recv.at[0],
    )
    p_along, p_across = axis_gather(p_cols, 8, 1)
    one()
    start(p_first)
    two()
    p_swap.start()
    receive(p_first)
    start(p_second)
    three()
    load.wait()

    def split_rows(index, carry):
        rows = pl.ds(pl.multiple_of(index * 64, 64), 64)
        a_high[rows, :], a_low[rows, :] = split(a_full[rows, :])
        return carry

    lax.fori_loop(0, ROW_BLOCK // 64, split_rows, 0)
    gram_all()
    p_swap.receive()
    p_along.start()
    factor(work_one, g_all[...])
    first_out[...] = work_one[:, :NB]
    inverse = work_one[:, NB:]
    receive(p_second)

    def basis_rows(index, carry):
        rows = pl.ds(pl.multiple_of(index * WIDE, WIDE), WIDE)
        value = dot(p_rows[index].reshape(WIDE, NB), inverse, ((1,), (1,)))
        q_rows[rows, :] = value
        high, low = split(value.T)
        q_wide[:NB, rows] = high
        q_wide[NB:, rows] = low
        return carry

    lax.fori_loop(0, SIDE, basis_rows, 0)
    mine = q_rows[pl.ds(pl.multiple_of(me_c * SHARD, SHARD), SHARD), :]
    h_own[...] = dot(mine, mine, ((0,), (0,)))
    one, two, three, more_all, more_finish = summed(h_own, h_buf, h_part, h_all, 1)
    one()
    p_along.receive()
    p_across.start()

    piece = lambda place, k: pl.ds(pl.multiple_of((2 * place + k) * SHARD, SHARD), SHARD)
    y_pair = [
        pltpu.make_async_remote_copy(
            src_ref=y_part.at[piece(k, 1 - core), :], dst_ref=y_mate.at[k],
            send_sem=one_send.at[4 + k], recv_sem=one_recv.at[4 + k],
            device_id=mate, device_id_type=MESH,
        )
        for k in range(SIDE)
    ]

    def products(index, carry):
        cols = pl.ds(pl.multiple_of(index * TILE // 2, TILE // 2), TILE // 2)
        wide = dot(q_wide[...], a_high[:, cols], ((1,), (0,)), None)
        value = wide[:NB, :] + wide[NB:, :]
        value = value + dot(q_wide[:NB, :], a_low[:, cols], ((1,), (0,)), None)
        y_part[cols, :] = value.T
        return carry

    for half in range(2):
        lax.fori_loop(5 * half, 5 * half + 5, products, 0)
        y_pair[2 * half].start()
        y_pair[2 * half + 1].start()
    two()

    def basis_cols(index, carry):
        rows = pl.ds(pl.multiple_of(index * 2 * SHARD, 2 * SHARD), 2 * SHARD)
        q_cols[rows, :] = dot(p_cols[index].reshape(2 * SHARD, NB), inverse, ((1,), (1,)))
        return carry

    p_across.receive()
    lax.fori_loop(0, SIDE, basis_cols, 0)
    s_own[...] = dot3(q_cols[...], y_part[...], ((0,), (0,)))
    center_one, center_two, center_three, center_all, center_finish = summed(
        s_own, s_buf, s_part, s_all, 2
    )
    center_one()
    for k in range(SIDE):
        y_pair[k].wait_recv()
        y_half[k] = y_part[piece(k, core), :] + y_mate[k]
    y_along = ring(in_z, z, lambda peer: y_half.at[peer], lambda slot: y_ring.at[slot], 9)
    y_along.start()
    three()
    y_ring[z] = y_half[z]
    y_along.receive()
    y_cols[z, core] = y_ring[0] + y_ring[1] + (y_ring[2] + y_ring[3])
    y_first, y_second = plane_gather(y_rows, 4)
    y_swaps = [
        Swap(
            turned, (turn_r, turn_c), y_cols.at[z, core, pl.ds(half * HALF, HALF)],
            lambda slot, half=half: y_rows.at[slot // SIDE, lax.rem(slot, SIDE), half],
            turn_c, me_c, one_send.at[2 + half], one_recv.at[2 + half],
        )
        for half in range(2)
    ]
    y_columns, y_across = axis_gather(y_cols, 10, 8)
    start(y_swaps)
    y_columns.start()
    center_two()
    more_all()
    factor(work_two, h_all[...])
    receive(y_swaps)
    start(y_first)
    center_three()
    r_out[...] = dot(work_two[:, :NB], work_one[:, :NB], ((1,), (0,)))
    second = work_two[:, NB:]
    gram_inverse = dot(second, second, ((0,), (0,)))

    def finish_x(index, carry):
        rows = pl.ds(pl.multiple_of(index * WIDE, WIDE), WIDE)
        x_high[rows, :], x_low[rows, :] = split(dot3(q_rows[rows, :], gram_inverse, ((1,), (0,))))
        return carry

    lax.fori_loop(0, SIDE, finish_x, 0)
    receive(y_first)
    start(y_second)
    y_columns.receive()
    y_across.start()
    center_all()
    center = 4.0 * s_all[...]
    y_across.receive()

    def finish_right(index, carry):
        rows = pl.ds(pl.multiple_of(index * WIDE, WIDE), WIDE)
        half = pl.ds(2 * index, 2)
        x_tile = dot3(q_cols[rows, :], gram_inverse, ((1,), (0,)))
        mixed = 2.0 * y_cols[half].reshape(WIDE, NB) - dot3(x_tile, center, ((1,), (0,)))
        for target, value in ((mixed_t, mixed), (right, 2.0 * x_tile)):
            high, low = split(value.T)
            target[:NB, rows] = high
            target[NB : 2 * NB, rows] = low
            target[2 * NB :, rows] = high
        return carry

    lax.fori_loop(0, 2, finish_right, 0)

    def update_x(index, carry):
        rows = pl.ds(pl.multiple_of(index * TILE, TILE), TILE)
        high = x_high[rows, :]
        wide = jnp.concatenate([high, high, x_low[rows, :]], axis=1)
        a_full[rows, :] = a_full[rows, :] - dot(wide, mixed_t[...], ((1,), (0,)), None)
        return carry

    lax.fori_loop(0, ROW_BLOCK // TILE, update_x, 0)
    receive(y_second)

    def finish_y(index, carry):
        down, over = index // SIDE, lax.rem(index, SIDE)
        same = over // 2 == core
        source_x = jnp.where(same, over, SIDE - 1 - over)
        source_core = jnp.where(same, core, 1 - core)
        rank = lax.rem(source_x, 2) * ROWS + 2 * down + source_core
        rows = pl.ds(pl.multiple_of(rank * SHARD, SHARD), SHARD)
        left_high[rows, :], left_low[rows, :] = split(y_rows[down, over].reshape(SHARD, NB))
        return carry

    lax.fori_loop(0, COLS, finish_y, 0)

    gram_finish()
    more_finish()
    center_finish()
    for item in (*p_first, *p_second, p_swap, p_along, p_across, y_along):
        item.finish()
    for item in (*y_swaps, *y_first, *y_second, y_columns, y_across):
        item.finish()
    for item in y_pair:
        item.wait_send()


def panel_call(trailing, panel_block):
    vmem = pl.BlockSpec(memory_space=pltpu.VMEM)
    f32 = lambda *dims: pltpu.VMEM(dims, F32)
    bf16 = lambda *dims: pltpu.VMEM(dims, BF16)
    dma = lambda *dims: pltpu.SemaphoreType.DMA(dims)
    left, small = bf16(ROW_BLOCK, NB), f32(NB, NB)
    right = bf16(3 * NB, COL_BLOCK)
    plane = f32(SIDE, SIDE, 2, HALF, NB)
    axis = f32(SIDE, 2, SHARD, NB)
    ring = f32(SIDE, SHARD, NB)
    return pl.pallas_call(
        panel_kernel,
        out_shape=[f32(ROW_BLOCK, COL_BLOCK), left, left, right, small, small],
        in_specs=[pl.BlockSpec(memory_space=pl.ANY)] * 2,
        out_specs=[vmem] * 6,
        scratch_shapes=[
            f32(SHARD, NB), left, left, right,
            bf16(ROW_BLOCK, COL_BLOCK), bf16(ROW_BLOCK, COL_BLOCK),
            plane, f32(ROW_BLOCK, NB), bf16(2 * NB, ROW_BLOCK), axis, f32(COL_BLOCK, NB),
            f32(COL_BLOCK, NB), ring, ring, ring, axis, plane,
            *(3 * [small, small, f32(8 * ROWS, NB), small]),
            f32(NB, 2 * NB), f32(NB, 2 * NB),
            pltpu.SemaphoreType.DMA, pltpu.SemaphoreType.DMA, dma(6, COLS), dma(6, COLS), dma(3, ROWS), dma(3, ROWS),
            dma(11, SIDE), dma(11, SIDE), dma(9), dma(9),
        ],
        compiler_params=pltpu.CompilerParams(
            collective_id=0, has_side_effects=True, vmem_limit_bytes=36 * 1024 * 1024
        ),
        name="panel",
    )(trailing, pltpu.with_memory_space_constraint(panel_block, pltpu.HBM))


def update_kernel(
    trailing, left_high, left_low, right, r_in, first_in, out, r_out, first_out, ready, sems
):
    def send(index, slot):
        rows = pl.ds(pl.multiple_of(index * TILE, TILE), TILE)
        return pltpu.make_async_copy(ready.at[slot], out.at[rows, :], sems.at[slot])

    def body(index, carry):
        slot = lax.rem(index, SLOTS)

        @pl.when(index >= SLOTS)
        def _():
            send(index - SLOTS, slot).wait()

        rows = pl.ds(pl.multiple_of(index * TILE, TILE), TILE)
        high = left_high[rows, :]
        left = jnp.concatenate([high, high, left_low[rows, :]], axis=1)
        ready[slot] = trailing[rows, :] - dot(left, right[...], ((1,), (0,)), None)
        send(index, slot).start()
        return carry

    count = ROW_BLOCK // TILE
    lax.fori_loop(0, count, body, 0)
    r_out[...] = r_in[...]
    first_out[...] = first_in[...]
    for index in range(count - SLOTS, count):
        send(index, index % SLOTS).wait()


def update_call(*pieces):
    vmem = pl.BlockSpec(memory_space=pltpu.VMEM)
    small = jax.ShapeDtypeStruct((NB, NB), F32)
    return pl.pallas_call(
        update_kernel,
        out_shape=[jax.ShapeDtypeStruct((ROW_BLOCK, COL_BLOCK), F32), small, small],
        in_specs=[vmem] * 6,
        out_specs=[pl.BlockSpec(memory_space=pltpu.HBM), vmem, vmem],
        scratch_shapes=[
            pltpu.VMEM((SLOTS, TILE, COL_BLOCK), F32), pltpu.SemaphoreType.DMA((SLOTS,))
        ],
        compiler_params=pltpu.CompilerParams(vmem_limit_bytes=8 * 1024 * 1024),
        name="update",
    )(*(pltpu.with_memory_space_constraint(piece, pltpu.VMEM) for piece in pieces))


def on_device(trailing, panel_block):
    pieces = panel_call(trailing, panel_block)
    return tuple(update_call(*pieces))


def solution(mesh):
    in_specs = (P("row", "col"), P(("row", "col"), None))
    out_specs = (P("row", "col"), P(), P())
    return jax.shard_map(
        on_device, mesh=mesh, in_specs=in_specs, out_specs=out_specs, check_vma=False
    )
```

```python
import jax
import jax.numpy as jnp
from jax import lax
from jax.experimental import pallas as pl
from jax.experimental.pallas import tpu as pltpu
from jax.sharding import PartitionSpec as P

HIGHEST = lax.Precision.HIGHEST
MESH = pl.DeviceIdType.MESH
F32 = jnp.float32
BF16 = jnp.bfloat16

ROWS = 8
COLS = 16
SIDE = 4
NB = 128
SHARD = 160
HALF = 80
ROW_BLOCK = SHARD * COLS
COL_BLOCK = SHARD * ROWS
TILE = 256
STEP = 32
SLOTS = 3
WIDE = SIDE * SHARD


def dot(first, second, contract, precision=HIGHEST):
    return lax.dot_general(
        first, second, (contract, ((), ())), precision=precision, preferred_element_type=F32
    )


def split(value):
    high = value.astype(BF16)
    return high, (value - high.astype(F32)).astype(BF16)


def dot3(first, second, contract):
    (a, b), (c, d) = split(first), split(second)
    value = dot(a, c, contract, None)
    return value + (dot(a, d, contract, None) + dot(b, c, contract, None))


def factor(work, gram=None, bases=range(0, NB, STEP)):
    step = STEP
    down = lax.broadcasted_iota(jnp.int32, (NB, NB), 0)
    across = lax.broadcasted_iota(jnp.int32, (NB, NB), 1)
    if gram is not None:
        work[:, :NB] = gram
        work[:, NB:] = jnp.where(down == across, 1.0, 0.0)
    sub = lax.broadcasted_iota(jnp.int32, (step, 1), 0)
    for base in bases:
        rows = work[base : base + step, :]
        tall = [
            jnp.broadcast_to(rows[:, base + k : base + k + 1], (step, NB)) for k in range(step)
        ]
        for k in range(step):
            scale = lax.rsqrt(tall[k][k : k + 1, :])
            low = tall[k] * scale
            for m in range(k + 1, step):
                tall[m] = tall[m] - low * low[m : m + 1, :]
            top = rows[k : k + 1, :] * jnp.concatenate([scale, scale], axis=1)
            low = jnp.where(sub > k, low, 0.0)
            rows = jnp.where(sub == k, top, rows - jnp.concatenate([low, low], axis=1) * top)
        work[base : base + step, :] = rows
        if base + step < NB:
            change = dot(rows[:, :NB], rows, ((0,), (0,)))
            work[base + step :, :] = work[base + step :, :] - change[base + step :, :]
    if bases[-1] == NB - step:
        work[:, :NB] = jnp.where(across >= down, work[:, :NB], 0.0)
        work[:, NB:] = jnp.where(across <= down, work[:, NB:], 0.0)


class Exchange:
    def __init__(self, size, me, place, source, target, send_sem, recv_sem):
        self.size, self.me, self.place = size, me, place
        self.source, self.target = source, target
        self.send_sem, self.recv_sem = send_sem, recv_sem

    def each(self, action, unroll=False):
        def body(step, carry):
            action(lax.rem(self.me + step, self.size))
            return carry

        if unroll or self.size == SIDE:
            for step in range(1, self.size):
                body(step, 0)
        else:
            lax.fori_loop(1, self.size, body, 0)

    def copy(self, peer, slot):
        return pltpu.make_async_remote_copy(
            src_ref=self.source(peer),
            dst_ref=self.target(slot),
            send_sem=self.send_sem.at[peer],
            recv_sem=self.recv_sem.at[slot],
            device_id=self.place(peer),
            device_id_type=MESH,
        )

    def start(self):
        self.each(lambda peer: self.copy(peer, self.me).start(), unroll=True)

    def receive(self):
        self.each(lambda peer: self.copy(peer, peer).wait_recv())

    def finish(self):
        self.each(lambda peer: self.copy(peer, peer).wait_send())


class Swap:
    def __init__(self, apart, place, source, target, there, here, send_sem, recv_sem):
        self.apart, self.here, self.source, self.target = apart, here, source, target
        self.copy = lambda slot: pltpu.make_async_remote_copy(
            src_ref=source, dst_ref=target(slot), send_sem=send_sem, recv_sem=recv_sem,
            device_id=place, device_id_type=MESH,
        )
        self.there = there

    def start(self):
        @pl.when(self.apart)
        def _():
            self.copy(self.there).start()

        @pl.when(jnp.logical_not(self.apart))
        def _():
            self.target(self.here)[...] = self.source[...]

    def receive(self):
        @pl.when(self.apart)
        def _():
            self.copy(self.here).wait_recv()

    def finish(self):
        @pl.when(self.apart)
        def _():
            self.copy(self.there).wait_send()


def eights(ref):
    return lambda index: ref.at[pl.ds(pl.multiple_of(index * 8, 8), 8), :]


def panel_kernel(
    trailing_hbm, panel_hbm,
    a_full, left_high, left_low, right, r_out, first_out,
    panel, x_high, x_low, mixed_t, a_high, a_low, p_rows, q_rows, q_wide, p_cols, q_cols,
    y_part, y_mate, y_half, y_ring, y_cols, y_rows,
    g_own, g_buf, g_part, g_all, h_own, h_buf, h_part, h_all, s_own, s_buf, s_part, s_all,
    work_one, work_two,
    a_sem, panel_sem, plane_send, plane_recv, axis_send, axis_recv, ring_send, ring_recv, one_send, one_recv,
):
    me_r, me_c = lax.axis_index("row"), lax.axis_index("col")
    z, core = me_r // 2, lax.rem(me_r, 2)
    y, x = me_c // SIDE, lax.rem(me_c, SIDE)
    in_plane = lambda peer: (me_r, peer)
    in_axis = lambda peer: (peer, me_c)
    in_x = lambda peer: (me_r, y * SIDE + peer)
    in_y = lambda peer: (me_r, peer * SIDE + x)
    in_z = lambda peer: (2 * peer + core, me_c)
    mate = (2 * z + 1 - core, me_c)
    out_r, out_c = lax.rem(me_c, ROWS), 2 * me_r + me_c // ROWS
    in_r, in_c = me_c // 2, ROWS * lax.rem(me_c, 2) + me_r
    apart = jnp.logical_not(jnp.logical_and(out_r == me_r, out_c == me_c))
    straight = core == x // 2
    turn_r = 2 * y + jnp.where(straight, core, 1 - core)
    turn_c = z * SIDE + jnp.where(straight, x, SIDE - 1 - x)
    turned = jnp.logical_not(jnp.logical_and(straight, y == z))

    fetch = pltpu.make_async_copy(panel_hbm, panel, panel_sem)
    fetch.start()
    load = pltpu.make_async_copy(trailing_hbm, a_full, a_sem)
    load.start()
    barrier = pltpu.get_barrier_semaphore()

    def signal(place):
        pl.semaphore_signal(barrier, inc=1, device_id=place, device_id_type=MESH)

    def greet(size, me, place):
        def body(step, carry):
            signal(place(lax.rem(me + step, size)))
            return carry

        lax.fori_loop(1, size, body, 0)

    greet(COLS, me_c, in_plane)
    greet(ROWS, me_r, in_axis)

    @pl.when(apart)
    def _():
        signal((out_r, out_c))
        signal((in_r, in_c))

    @pl.when(turned)
    def _():
        signal((turn_r, turn_c))

    fetch.wait()
    g_own[...] = dot(panel[...], panel[...], ((0,), (0,)))
    for half in range(2):
        p_rows[y, x, half] = panel[half * HALF : (half + 1) * HALF, :]
    pl.semaphore_wait(
        barrier, COLS + ROWS - 2 + jnp.where(apart, 2, 0) + jnp.where(turned, 1, 0)
    )

    def summed(own, buf, part, full, sem):
        scatter = Exchange(
            COLS, me_c, in_plane, eights(own), eights(buf),
            plane_send.at[sem], plane_recv.at[sem],
        )
        share = Exchange(
            ROWS, me_r, in_axis, lambda peer: eights(part)(me_r), eights(part),
            axis_send.at[sem], axis_recv.at[sem],
        )
        gather = Exchange(
            COLS, me_c, in_plane, lambda peer: eights(full)(me_c), eights(full),
            plane_send.at[sem + 3], plane_recv.at[sem + 3],
        )

        def total(source, count):
            value = source[:8, :]
            for k in range(1, count):
                value = value + source[k * 8 : k * 8 + 8, :]
            return value

        def one():
            eights(buf)(me_c)[...] = eights(own)(me_c)[...]
            scatter.start()

        def two():
            scatter.receive()
            eights(part)(me_r)[...] = total(buf, COLS)
            share.start()

        def three():
            share.receive()
            eights(full)(me_c)[...] = total(part, ROWS)
            gather.start()

        def finish():
            scatter.finish()
            share.finish()
            gather.finish()

        return one, two, three, gather.receive, finish

    def ring(place, me, source, target, sem):
        return Exchange(SIDE, me, place, source, target, ring_send.at[sem], ring_recv.at[sem])

    def plane_gather(rows, sem):
        first = (
            ring(in_y, y, lambda peer: rows.at[y, x, 0], lambda slot: rows.at[slot, x, 0], sem),
            ring(in_x, x, lambda peer: rows.at[y, x, 1], lambda slot: rows.at[y, slot, 1], sem + 1),
        )
        second = (
            ring(in_x, x, lambda peer: rows.at[:, x, 0], lambda slot: rows.at[:, slot, 0], sem + 2),
            ring(in_y, y, lambda peer: rows.at[y, :, 1], lambda slot: rows.at[slot, :, 1], sem + 3),
        )
        return first, second

    def start(pair):
        for item in pair:
            item.start()

    def receive(pair):
        for item in pair:
            item.receive()

    def axis_gather(cols, sem, mate_sem):
        along = ring(
            in_z, z, lambda peer: cols.at[z, core], lambda slot: cols.at[slot, core], sem
        )
        across = Swap(
            True, mate, cols.at[:, core], lambda slot: cols.at[:, slot], core, 1 - core,
            one_send.at[mate_sem], one_recv.at[mate_sem],
        )
        return along, across

    one, two, three, gram_all, gram_finish = summed(g_own, g_buf, g_part, g_all, 0)
    p_first, p_second = plane_gather(p_rows, 0)
    p_swap = Swap(
        apart, (out_r, out_c), panel, lambda slot: p_cols.at[slot // 2, lax.rem(slot, 2)],
        out_r, me_r, one_send.at[0], one_recv.at[0],
    )
    p_along, p_across = axis_gather(p_cols, 8, 1)
    one()
    start(p_first)
    two()
    p_swap.start()
    receive(p_first)
    start(p_second)
    three()
    load.wait()

    def split_rows(index, carry):
        rows = pl.ds(pl.multiple_of(index * 64, 64), 64)
        a_high[rows, :], a_low[rows, :] = split(a_full[rows, :])
        return carry

    lax.fori_loop(0, ROW_BLOCK // 64, split_rows, 0)
    gram_all()
    p_swap.receive()
    p_along.start()
    factor(work_one, g_all[...])
    first_out[...] = work_one[:, :NB]
    inverse = work_one[:, NB:]
    receive(p_second)

    def basis_rows(index, carry):
        rows = pl.ds(pl.multiple_of(index * WIDE, WIDE), WIDE)
        value = dot(p_rows[index].reshape(WIDE, NB), inverse, ((1,), (1,)))
        q_rows[rows, :] = value
        high, low = split(value.T)
        q_wide[:NB, rows] = high
        q_wide[NB:, rows] = low
        return carry

    lax.fori_loop(0, SIDE, basis_rows, 0)
    mine = q_rows[pl.ds(pl.multiple_of(me_c * SHARD, SHARD), SHARD), :]
    h_own[...] = dot(mine, mine, ((0,), (0,)))
    one, two, three, more_all, more_finish = summed(h_own, h_buf, h_part, h_all, 1)
    one()
    p_along.receive()
    p_across.start()

    piece = lambda place, k: pl.ds(pl.multiple_of((2 * place + k) * SHARD, SHARD), SHARD)
    y_pair = [
        pltpu.make_async_remote_copy(
            src_ref=y_part.at[piece(k, 1 - core), :], dst_ref=y_mate.at[k],
            send_sem=one_send.at[4 + k], recv_sem=one_recv.at[4 + k],
            device_id=mate, device_id_type=MESH,
        )
        for k in range(SIDE)
    ]

    def products(index, carry):
        cols = pl.ds(pl.multiple_of(index * TILE, TILE), TILE)
        wide = dot(q_wide[...], a_high[:, cols], ((1,), (0,)), None)
        value = wide[:NB, :] + wide[NB:, :]
        value = value + dot(q_wide[:NB, :], a_low[:, cols], ((1,), (0,)), None)
        y_part[cols, :] = value.T
        return carry

    for half, (begin, end) in enumerate(((0, 3), (3, 5))):
        lax.fori_loop(begin, end, products, 0)
        y_pair[2 * half].start()
        y_pair[2 * half + 1].start()
    two()

    def basis_cols(index, carry):
        rows = pl.ds(pl.multiple_of(index * 2 * SHARD, 2 * SHARD), 2 * SHARD)
        q_cols[rows, :] = dot(p_cols[index].reshape(2 * SHARD, NB), inverse, ((1,), (1,)))
        return carry

    p_across.receive()
    lax.fori_loop(0, SIDE, basis_cols, 0)
    s_own[...] = dot3(q_cols[...], y_part[...], ((0,), (0,)))
    center_one, center_two, center_three, center_all, center_finish = summed(
        s_own, s_buf, s_part, s_all, 2
    )
    center_one()
    for k in range(SIDE):
        y_pair[k].wait_recv()
        y_half[k] = y_part[piece(k, core), :] + y_mate[k]
    y_along = ring(in_z, z, lambda peer: y_half.at[peer], lambda slot: y_ring.at[slot], 9)
    y_along.start()
    three()
    y_ring[z] = y_half[z]
    gram_finish()
    for item in (*p_first, *p_second, p_swap, p_along):
        item.finish()
    y_along.receive()
    y_cols[z, core] = y_ring[0] + y_ring[1] + (y_ring[2] + y_ring[3])
    y_first, y_second = plane_gather(y_rows, 4)
    y_swaps = [
        Swap(
            turned, (turn_r, turn_c), y_cols.at[z, core, pl.ds(half * HALF, HALF)],
            lambda slot, half=half: y_rows.at[slot // SIDE, lax.rem(slot, SIDE), half],
            turn_c, me_c, one_send.at[2 + half], one_recv.at[2 + half],
        )
        for half in range(2)
    ]
    y_columns, y_across = axis_gather(y_cols, 10, 8)
    start(y_swaps)
    y_columns.start()
    center_two()
    more_all()
    factor(work_two, h_all[...])
    receive(y_swaps)
    start(y_first)
    center_three()
    r_out[...] = dot(work_two[:, :NB], work_one[:, :NB], ((1,), (0,)))
    second = work_two[:, NB:]
    gram_inverse = dot(second, second, ((0,), (0,)))

    def finish_x(index, carry):
        rows = pl.ds(pl.multiple_of(index * WIDE, WIDE), WIDE)
        x_high[rows, :], x_low[rows, :] = split(dot3(q_rows[rows, :], gram_inverse, ((1,), (0,))))
        return carry

    lax.fori_loop(0, SIDE, finish_x, 0)
    receive(y_first)
    start(y_second)
    y_columns.receive()
    y_across.start()
    center_all()
    center = 4.0 * s_all[...]
    y_across.receive()

    def finish_right(index, carry):
        rows = pl.ds(pl.multiple_of(index * WIDE, WIDE), WIDE)
        half = pl.ds(2 * index, 2)
        x_tile = dot3(q_cols[rows, :], gram_inverse, ((1,), (0,)))
        mixed = 2.0 * y_cols[half].reshape(WIDE, NB) - dot3(x_tile, center, ((1,), (0,)))
        for target, value in ((mixed_t, mixed), (right, 2.0 * x_tile)):
            high, low = split(value.T)
            target[:NB, rows] = high
            target[NB : 2 * NB, rows] = low
            target[2 * NB :, rows] = high
        return carry

    lax.fori_loop(0, 2, finish_right, 0)

    def update_x(index, carry):
        rows = pl.ds(pl.multiple_of(index * TILE, TILE), TILE)
        high = x_high[rows, :]
        wide = jnp.concatenate([high, high, x_low[rows, :]], axis=1)
        a_full[rows, :] = a_full[rows, :] - dot(wide, mixed_t[...], ((1,), (0,)), None)
        return carry

    lax.fori_loop(0, ROW_BLOCK // TILE, update_x, 0)
    more_finish()
    center_finish()
    for item in (p_across, y_along, *y_swaps, *y_first, y_columns):
        item.finish()
    for item in y_pair:
        item.wait_send()
    receive(y_second)

    def finish_y(index, carry):
        down, over = index // SIDE, lax.rem(index, SIDE)
        same = over // 2 == core
        source_x = jnp.where(same, over, SIDE - 1 - over)
        source_core = jnp.where(same, core, 1 - core)
        rank = lax.rem(source_x, 2) * ROWS + 2 * down + source_core
        rows = pl.ds(pl.multiple_of(rank * SHARD, SHARD), SHARD)
        left_high[rows, :], left_low[rows, :] = split(y_rows[down, over].reshape(SHARD, NB))
        return carry

    lax.fori_loop(0, COLS, finish_y, 0)

    for item in (*y_second, y_across):
        item.finish()


def panel_call(trailing, panel_block):
    vmem = pl.BlockSpec(memory_space=pltpu.VMEM)
    f32 = lambda *dims: pltpu.VMEM(dims, F32)
    bf16 = lambda *dims: pltpu.VMEM(dims, BF16)
    dma = lambda *dims: pltpu.SemaphoreType.DMA(dims)
    left, small = bf16(ROW_BLOCK, NB), f32(NB, NB)
    right = bf16(3 * NB, COL_BLOCK)
    plane = f32(SIDE, SIDE, 2, HALF, NB)
    axis = f32(SIDE, 2, SHARD, NB)
    ring = f32(SIDE, SHARD, NB)
    return pl.pallas_call(
        panel_kernel,
        out_shape=[f32(ROW_BLOCK, COL_BLOCK), left, left, right, small, small],
        in_specs=[pl.BlockSpec(memory_space=pl.ANY)] * 2,
        out_specs=[vmem] * 6,
        scratch_shapes=[
            f32(SHARD, NB), left, left, right,
            bf16(ROW_BLOCK, COL_BLOCK), bf16(ROW_BLOCK, COL_BLOCK),
            plane, f32(ROW_BLOCK, NB), bf16(2 * NB, ROW_BLOCK), axis, f32(COL_BLOCK, NB),
            f32(COL_BLOCK, NB), ring, ring, ring, axis, plane,
            *(3 * [small, small, f32(8 * ROWS, NB), small]),
            f32(NB, 2 * NB), f32(NB, 2 * NB),
            pltpu.SemaphoreType.DMA, pltpu.SemaphoreType.DMA, dma(6, COLS), dma(6, COLS), dma(3, ROWS), dma(3, ROWS),
            dma(11, SIDE), dma(11, SIDE), dma(9), dma(9),
        ],
        compiler_params=pltpu.CompilerParams(
            collective_id=0, has_side_effects=True, vmem_limit_bytes=36 * 1024 * 1024
        ),
        name="panel",
    )(trailing, pltpu.with_memory_space_constraint(panel_block, pltpu.HBM))


def update_kernel(
    trailing, left_high, left_low, right, r_in, first_in, out, r_out, first_out, ready, sems
):
    def send(index, slot):
        rows = pl.ds(pl.multiple_of(index * TILE, TILE), TILE)
        return pltpu.make_async_copy(ready.at[slot], out.at[rows, :], sems.at[slot])

    def body(index, carry):
        slot = lax.rem(index, SLOTS)

        @pl.when(index >= SLOTS)
        def _():
            send(index - SLOTS, slot).wait()

        rows = pl.ds(pl.multiple_of(index * TILE, TILE), TILE)
        high = left_high[rows, :]
        left = jnp.concatenate([high, high, left_low[rows, :]], axis=1)
        ready[slot] = trailing[rows, :] - dot(left, right[...], ((1,), (0,)), None)
        send(index, slot).start()
        return carry

    count = ROW_BLOCK // TILE
    lax.fori_loop(0, count, body, 0)
    r_out[...] = r_in[...]
    first_out[...] = first_in[...]
    for index in range(count - SLOTS, count):
        send(index, index % SLOTS).wait()


def update_call(*pieces):
    vmem = pl.BlockSpec(memory_space=pltpu.VMEM)
    small = jax.ShapeDtypeStruct((NB, NB), F32)
    return pl.pallas_call(
        update_kernel,
        out_shape=[jax.ShapeDtypeStruct((ROW_BLOCK, COL_BLOCK), F32), small, small],
        in_specs=[vmem] * 6,
        out_specs=[pl.BlockSpec(memory_space=pltpu.HBM), vmem, vmem],
        scratch_shapes=[
            pltpu.VMEM((SLOTS, TILE, COL_BLOCK), F32), pltpu.SemaphoreType.DMA((SLOTS,))
        ],
        compiler_params=pltpu.CompilerParams(vmem_limit_bytes=8 * 1024 * 1024),
        name="update",
    )(*(pltpu.with_memory_space_constraint(piece, pltpu.VMEM) for piece in pieces))


def on_device(trailing, panel_block):
    pieces = panel_call(trailing, panel_block)
    return tuple(update_call(*pieces))


def solution(mesh):
    in_specs = (P("row", "col"), P(("row", "col"), None))
    out_specs = (P("row", "col"), P(), P())
    return jax.shard_map(
        on_device, mesh=mesh, in_specs=in_specs, out_specs=out_specs, check_vma=False
    )
```

```python
import jax
import jax.numpy as jnp
from jax import lax
from jax.experimental import pallas as pl
from jax.experimental.pallas import tpu as pltpu
from jax.sharding import PartitionSpec as P

HIGHEST = lax.Precision.HIGHEST
MESH = pl.DeviceIdType.MESH
F32 = jnp.float32
BF16 = jnp.bfloat16

ROWS = 8
COLS = 16
SIDE = 4
NB = 128
SHARD = 160
HALF = 80
ROW_BLOCK = SHARD * COLS
COL_BLOCK = SHARD * ROWS
TILE = 256
STEP = 32
SLOTS = 3
WIDE = SIDE * SHARD


def dot(first, second, contract, precision=HIGHEST):
    return lax.dot_general(
        first, second, (contract, ((), ())), precision=precision, preferred_element_type=F32
    )


def split(value):
    high = value.astype(BF16)
    return high, (value - high.astype(F32)).astype(BF16)


def dot3(first, second, contract):
    (a, b), (c, d) = split(first), split(second)
    value = dot(a, c, contract, None)
    return value + (dot(a, d, contract, None) + dot(b, c, contract, None))


def factor(work, gram=None, bases=range(0, NB, STEP)):
    step = STEP
    down = lax.broadcasted_iota(jnp.int32, (NB, NB), 0)
    across = lax.broadcasted_iota(jnp.int32, (NB, NB), 1)
    if gram is not None:
        work[:, :NB] = gram
        work[:, NB:] = jnp.where(down == across, 1.0, 0.0)
    sub = lax.broadcasted_iota(jnp.int32, (step, 1), 0)
    for base in bases:
        rows = work[base : base + step, :]
        tall = [
            jnp.broadcast_to(rows[:, base + k : base + k + 1], (step, NB)) for k in range(step)
        ]
        for k in range(step):
            scale = lax.rsqrt(tall[k][k : k + 1, :])
            low = tall[k] * scale
            for m in range(k + 1, step):
                tall[m] = tall[m] - low * low[m : m + 1, :]
            top = rows[k : k + 1, :] * jnp.concatenate([scale, scale], axis=1)
            low = jnp.where(sub > k, low, 0.0)
            rows = jnp.where(sub == k, top, rows - jnp.concatenate([low, low], axis=1) * top)
        work[base : base + step, :] = rows
        if base + step < NB:
            change = dot(rows[:, :NB], rows, ((0,), (0,)))
            work[base + step :, :] = work[base + step :, :] - change[base + step :, :]
    if bases[-1] == NB - step:
        work[:, :NB] = jnp.where(across >= down, work[:, :NB], 0.0)
        work[:, NB:] = jnp.where(across <= down, work[:, NB:], 0.0)


class Exchange:
    def __init__(self, size, me, place, source, target, send_sem, recv_sem):
        self.size, self.me, self.place = size, me, place
        self.source, self.target = source, target
        self.send_sem, self.recv_sem = send_sem, recv_sem

    def each(self, action, unroll=False):
        def body(step, carry):
            action(lax.rem(self.me + step, self.size))
            return carry

        if unroll or self.size == SIDE:
            for step in range(1, self.size):
                body(step, 0)
        else:
            lax.fori_loop(1, self.size, body, 0)

    def copy(self, peer, slot):
        return pltpu.make_async_remote_copy(
            src_ref=self.source(peer),
            dst_ref=self.target(slot),
            send_sem=self.send_sem.at[peer],
            recv_sem=self.recv_sem.at[slot],
            device_id=self.place(peer),
            device_id_type=MESH,
        )

    def start(self):
        self.each(lambda peer: self.copy(peer, self.me).start(), unroll=True)

    def receive(self):
        self.each(lambda peer: self.copy(peer, peer).wait_recv(), unroll=True)

    def finish(self):
        self.each(lambda peer: self.copy(peer, peer).wait_send())


class Swap:
    def __init__(self, apart, place, source, target, there, here, send_sem, recv_sem):
        self.apart, self.here, self.source, self.target = apart, here, source, target
        self.copy = lambda slot: pltpu.make_async_remote_copy(
            src_ref=source, dst_ref=target(slot), send_sem=send_sem, recv_sem=recv_sem,
            device_id=place, device_id_type=MESH,
        )
        self.there = there

    def start(self):
        @pl.when(self.apart)
        def _():
            self.copy(self.there).start()

        @pl.when(jnp.logical_not(self.apart))
        def _():
            self.target(self.here)[...] = self.source[...]

    def receive(self):
        @pl.when(self.apart)
        def _():
            self.copy(self.here).wait_recv()

    def finish(self):
        @pl.when(self.apart)
        def _():
            self.copy(self.there).wait_send()


def eights(ref):
    return lambda index: ref.at[pl.ds(pl.multiple_of(index * 8, 8), 8), :]


def panel_kernel(
    trailing_hbm, panel_hbm,
    a_full, left_high, left_low, right, r_out, first_out,
    panel, x_high, x_low, mixed_t, a_high, a_low, p_rows, q_rows, q_wide, p_cols, q_cols,
    y_part, y_mate, y_half, y_ring, y_cols, y_rows,
    g_own, g_buf, g_part, g_all, h_own, h_buf, h_part, h_all, s_own, s_buf, s_part, s_all,
    work_one, work_two,
    a_sem, panel_sem, plane_send, plane_recv, axis_send, axis_recv, ring_send, ring_recv, one_send, one_recv,
):
    me_r, me_c = lax.axis_index("row"), lax.axis_index("col")
    z, core = me_r // 2, lax.rem(me_r, 2)
    y, x = me_c // SIDE, lax.rem(me_c, SIDE)
    in_plane = lambda peer: (me_r, peer)
    in_axis = lambda peer: (peer, me_c)
    in_x = lambda peer: (me_r, y * SIDE + peer)
    in_y = lambda peer: (me_r, peer * SIDE + x)
    in_z = lambda peer: (2 * peer + core, me_c)
    mate = (2 * z + 1 - core, me_c)
    out_r, out_c = lax.rem(me_c, ROWS), 2 * me_r + me_c // ROWS
    in_r, in_c = me_c // 2, ROWS * lax.rem(me_c, 2) + me_r
    apart = jnp.logical_not(jnp.logical_and(out_r == me_r, out_c == me_c))
    straight = core == x // 2
    turn_r = 2 * y + jnp.where(straight, core, 1 - core)
    turn_c = z * SIDE + jnp.where(straight, x, SIDE - 1 - x)
    turned = jnp.logical_not(jnp.logical_and(straight, y == z))

    fetch = pltpu.make_async_copy(panel_hbm, panel, panel_sem)
    fetch.start()
    load = pltpu.make_async_copy(trailing_hbm, a_full, a_sem)
    load.start()
    barrier = pltpu.get_barrier_semaphore()

    def signal(place):
        pl.semaphore_signal(barrier, inc=1, device_id=place, device_id_type=MESH)

    def greet(size, me, place):
        for step in range(1, size):
            signal(place(lax.rem(me + step, size)))

    greet(COLS, me_c, in_plane)
    greet(ROWS, me_r, in_axis)

    @pl.when(apart)
    def _():
        signal((out_r, out_c))
        signal((in_r, in_c))

    @pl.when(turned)
    def _():
        signal((turn_r, turn_c))

    fetch.wait()
    g_own[...] = dot(panel[...], panel[...], ((0,), (0,)))
    for half in range(2):
        p_rows[y, x, half] = panel[half * HALF : (half + 1) * HALF, :]
    pl.semaphore_wait(
        barrier, COLS + ROWS - 2 + jnp.where(apart, 2, 0) + jnp.where(turned, 1, 0)
    )

    def summed(own, buf, part, full, sem):
        scatter = Exchange(
            COLS, me_c, in_plane, eights(own), eights(buf),
            plane_send.at[sem], plane_recv.at[sem],
        )
        share = Exchange(
            ROWS, me_r, in_axis, lambda peer: eights(part)(me_r), eights(part),
            axis_send.at[sem], axis_recv.at[sem],
        )
        gather = Exchange(
            COLS, me_c, in_plane, lambda peer: eights(full)(me_c), eights(full),
            plane_send.at[sem + 3], plane_recv.at[sem + 3],
        )

        def total(source, count):
            value = source[:8, :]
            for k in range(1, count):
                value = value + source[k * 8 : k * 8 + 8, :]
            return value

        def one():
            eights(buf)(me_c)[...] = eights(own)(me_c)[...]
            scatter.start()

        def two():
            scatter.receive()
            eights(part)(me_r)[...] = total(buf, COLS)
            share.start()

        def three():
            share.receive()
            eights(full)(me_c)[...] = total(part, ROWS)
            gather.start()

        def finish():
            scatter.finish()
            share.finish()
            gather.finish()

        return one, two, three, gather.receive, finish

    def ring(place, me, source, target, sem):
        return Exchange(SIDE, me, place, source, target, ring_send.at[sem], ring_recv.at[sem])

    def plane_gather(rows, sem):
        first = (
            ring(in_y, y, lambda peer: rows.at[y, x, 0], lambda slot: rows.at[slot, x, 0], sem),
            ring(in_x, x, lambda peer: rows.at[y, x, 1], lambda slot: rows.at[y, slot, 1], sem + 1),
        )
        second = (
            ring(in_x, x, lambda peer: rows.at[:, x, 0], lambda slot: rows.at[:, slot, 0], sem + 2),
            ring(in_y, y, lambda peer: rows.at[y, :, 1], lambda slot: rows.at[slot, :, 1], sem + 3),
        )
        return first, second

    def start(pair):
        for item in pair:
            item.start()

    def receive(pair):
        for item in pair:
            item.receive()

    def axis_gather(cols, sem, mate_sem):
        along = ring(
            in_z, z, lambda peer: cols.at[z, core], lambda slot: cols.at[slot, core], sem
        )
        across = Swap(
            True, mate, cols.at[:, core], lambda slot: cols.at[:, slot], core, 1 - core,
            one_send.at[mate_sem], one_recv.at[mate_sem],
        )
        return along, across

    one, two, three, gram_all, gram_finish = summed(g_own, g_buf, g_part, g_all, 0)
    p_first, p_second = plane_gather(p_rows, 0)
    p_swap = Swap(
        apart, (out_r, out_c), panel, lambda slot: p_cols.at[slot // 2, lax.rem(slot, 2)],
        out_r, me_r, one_send.at[0], one_recv.at[0],
    )
    p_along, p_across = axis_gather(p_cols, 8, 1)
    start(p_first)
    one()
    two()
    p_swap.start()
    receive(p_first)
    start(p_second)
    three()
    load.wait()

    def split_rows(index, carry):
        rows = pl.ds(pl.multiple_of(index * 64, 64), 64)
        a_high[rows, :], a_low[rows, :] = split(a_full[rows, :])
        return carry

    lax.fori_loop(0, ROW_BLOCK // 64, split_rows, 0)
    gram_all()
    p_swap.receive()
    p_along.start()
    factor(work_one, g_all[...])
    first_out[...] = work_one[:, :NB]
    inverse = work_one[:, NB:]
    receive(p_second)

    def basis_rows(index, carry):
        rows = pl.ds(pl.multiple_of(index * WIDE, WIDE), WIDE)
        value = dot(p_rows[index].reshape(WIDE, NB), inverse, ((1,), (1,)))
        q_rows[rows, :] = value
        high, low = split(value.T)
        q_wide[:NB, rows] = high
        q_wide[NB:, rows] = low
        return carry

    lax.fori_loop(0, SIDE, basis_rows, 0)
    mine = q_rows[pl.ds(pl.multiple_of(me_c * SHARD, SHARD), SHARD), :]
    h_own[...] = dot(mine, mine, ((0,), (0,)))
    one, two, three, more_all, more_finish = summed(h_own, h_buf, h_part, h_all, 1)
    one()
    p_along.receive()
    p_across.start()

    piece = lambda place, k: pl.ds(pl.multiple_of((2 * place + k) * SHARD, SHARD), SHARD)
    y_pair = [
        pltpu.make_async_remote_copy(
            src_ref=y_part.at[piece(k, 1 - core), :], dst_ref=y_mate.at[k],
            send_sem=one_send.at[4 + k], recv_sem=one_recv.at[4 + k],
            device_id=mate, device_id_type=MESH,
        )
        for k in range(SIDE)
    ]

    def products(index, carry):
        cols = pl.ds(pl.multiple_of(index * TILE, TILE), TILE)
        wide = dot(q_wide[...], a_high[:, cols], ((1,), (0,)), None)
        value = wide[:NB, :] + wide[NB:, :]
        value = value + dot(q_wide[:NB, :], a_low[:, cols], ((1,), (0,)), None)
        y_part[cols, :] = value.T
        return carry

    for half, (begin, end) in enumerate(((0, 3), (3, 5))):
        lax.fori_loop(begin, end, products, 0)
        y_pair[2 * half].start()
        y_pair[2 * half + 1].start()
    two()

    def basis_cols(index, carry):
        rows = pl.ds(pl.multiple_of(index * 2 * SHARD, 2 * SHARD), 2 * SHARD)
        q_cols[rows, :] = dot(p_cols[index].reshape(2 * SHARD, NB), inverse, ((1,), (1,)))
        return carry

    p_across.receive()
    lax.fori_loop(0, SIDE, basis_cols, 0)
    s_own[...] = dot3(q_cols[...], y_part[...], ((0,), (0,)))
    center_one, center_two, center_three, center_all, center_finish = summed(
        s_own, s_buf, s_part, s_all, 2
    )
    center_one()
    for k in range(SIDE):
        y_pair[k].wait_recv()
        y_half[k] = y_part[piece(k, core), :] + y_mate[k]
    y_along = ring(in_z, z, lambda peer: y_half.at[peer], lambda slot: y_ring.at[slot], 9)
    y_along.start()
    three()
    center_two()
    y_ring[z] = y_half[z]
    gram_finish()
    for item in (*p_first, *p_second, p_swap, p_along):
        item.finish()
    y_along.receive()
    y_cols[z, core] = y_ring[0] + y_ring[1] + (y_ring[2] + y_ring[3])
    y_first, y_second = plane_gather(y_rows, 4)
    y_swaps = [
        Swap(
            turned, (turn_r, turn_c), y_cols.at[z, core, pl.ds(half * HALF, HALF)],
            lambda slot, half=half: y_rows.at[slot // SIDE, lax.rem(slot, SIDE), half],
            turn_c, me_c, one_send.at[2 + half], one_recv.at[2 + half],
        )
        for half in range(2)
    ]
    y_columns, y_across = axis_gather(y_cols, 10, 8)
    start(y_swaps)
    y_columns.start()
    more_all()
    factor(work_two, h_all[...])
    center_three()
    receive(y_swaps)
    start(y_first)
    second = work_two[:, NB:]
    gram_inverse = dot(second, second, ((0,), (0,)))

    def finish_x(index, carry):
        rows = pl.ds(pl.multiple_of(index * WIDE, WIDE), WIDE)
        x_high[rows, :], x_low[rows, :] = split(dot3(q_rows[rows, :], gram_inverse, ((1,), (0,))))
        return carry

    lax.fori_loop(0, SIDE, finish_x, 0)
    receive(y_first)
    start(y_second)
    y_columns.receive()
    y_across.start()
    center_all()
    center = 4.0 * s_all[...]
    y_across.receive()

    def finish_right(index, carry):
        rows = pl.ds(pl.multiple_of(index * WIDE, WIDE), WIDE)
        half = pl.ds(2 * index, 2)
        x_tile = dot3(q_cols[rows, :], gram_inverse, ((1,), (0,)))
        mixed = 2.0 * y_cols[half].reshape(WIDE, NB) - dot3(x_tile, center, ((1,), (0,)))
        for target, value in ((mixed_t, mixed), (right, 2.0 * x_tile)):
            high, low = split(value.T)
            target[:NB, rows] = high
            target[NB : 2 * NB, rows] = low
            target[2 * NB :, rows] = high
        return carry

    lax.fori_loop(0, 2, finish_right, 0)

    def update_x(index, carry):
        rows = pl.ds(pl.multiple_of(index * 2 * TILE, 2 * TILE), 2 * TILE)
        high = x_high[rows, :]
        wide = jnp.concatenate([high, high, x_low[rows, :]], axis=1)
        a_full[rows, :] = a_full[rows, :] - dot(wide, mixed_t[...], ((1,), (0,)), None)
        return carry

    lax.fori_loop(0, ROW_BLOCK // (2 * TILE), update_x, 0)
    r_out[...] = dot(work_two[:, :NB], work_one[:, :NB], ((1,), (0,)))
    more_finish()
    center_finish()
    for item in (p_across, y_along, *y_swaps, *y_first, y_columns):
        item.finish()
    for item in y_pair:
        item.wait_send()
    receive(y_second)

    def finish_y(index, carry):
        down, over = index // SIDE, lax.rem(index, SIDE)
        same = over // 2 == core
        source_x = jnp.where(same, over, SIDE - 1 - over)
        source_core = jnp.where(same, core, 1 - core)
        rank = lax.rem(source_x, 2) * ROWS + 2 * down + source_core
        rows = pl.ds(pl.multiple_of(rank * SHARD, SHARD), SHARD)
        left_high[rows, :], left_low[rows, :] = split(y_rows[down, over].reshape(SHARD, NB))
        return carry

    lax.fori_loop(0, COLS, finish_y, 0)

    for item in (*y_second, y_across):
        item.finish()


def panel_call(trailing, panel_block):
    vmem = pl.BlockSpec(memory_space=pltpu.VMEM)
    f32 = lambda *dims: pltpu.VMEM(dims, F32)
    bf16 = lambda *dims: pltpu.VMEM(dims, BF16)
    dma = lambda *dims: pltpu.SemaphoreType.DMA(dims)
    left, small = bf16(ROW_BLOCK, NB), f32(NB, NB)
    right = bf16(3 * NB, COL_BLOCK)
    plane = f32(SIDE, SIDE, 2, HALF, NB)
    axis = f32(SIDE, 2, SHARD, NB)
    ring = f32(SIDE, SHARD, NB)
    return pl.pallas_call(
        panel_kernel,
        out_shape=[f32(ROW_BLOCK, COL_BLOCK), left, left, right, small, small],
        in_specs=[pl.BlockSpec(memory_space=pl.ANY)] * 2,
        out_specs=[vmem] * 6,
        scratch_shapes=[
            f32(SHARD, NB), left, left, right,
            bf16(ROW_BLOCK, COL_BLOCK), bf16(ROW_BLOCK, COL_BLOCK),
            plane, f32(ROW_BLOCK, NB), bf16(2 * NB, ROW_BLOCK), axis, f32(COL_BLOCK, NB),
            f32(COL_BLOCK, NB), ring, ring, ring, axis, plane,
            *(3 * [small, small, f32(8 * ROWS, NB), small]),
            f32(NB, 2 * NB), f32(NB, 2 * NB),
            pltpu.SemaphoreType.DMA, pltpu.SemaphoreType.DMA, dma(6, COLS), dma(6, COLS), dma(3, ROWS), dma(3, ROWS),
            dma(11, SIDE), dma(11, SIDE), dma(9), dma(9),
        ],
        compiler_params=pltpu.CompilerParams(
            collective_id=0, has_side_effects=True, vmem_limit_bytes=36 * 1024 * 1024
        ),
        name="panel",
    )(trailing, pltpu.with_memory_space_constraint(panel_block, pltpu.HBM))


def update_kernel(
    trailing, left_high, left_low, right, r_in, first_in, out, r_out, first_out, ready, sems
):
    def send(index, slot):
        rows = pl.ds(pl.multiple_of(index * TILE, TILE), TILE)
        return pltpu.make_async_copy(ready.at[slot], out.at[rows, :], sems.at[slot])

    def body(index, carry):
        slot = lax.rem(index, SLOTS)

        @pl.when(index >= SLOTS)
        def _():
            send(index - SLOTS, slot).wait()

        rows = pl.ds(pl.multiple_of(index * TILE, TILE), TILE)
        high = left_high[rows, :]
        left = jnp.concatenate([high, high, left_low[rows, :]], axis=1)
        ready[slot] = trailing[rows, :] - dot(left, right[...], ((1,), (0,)), None)
        send(index, slot).start()
        return carry

    count = ROW_BLOCK // TILE
    lax.fori_loop(0, count, body, 0)
    r_out[...] = r_in[...]
    first_out[...] = first_in[...]
    for index in range(count - SLOTS, count):
        send(index, index % SLOTS).wait()


def update_call(*pieces):
    vmem = pl.BlockSpec(memory_space=pltpu.VMEM)
    small = jax.ShapeDtypeStruct((NB, NB), F32)
    return pl.pallas_call(
        update_kernel,
        out_shape=[jax.ShapeDtypeStruct((ROW_BLOCK, COL_BLOCK), F32), small, small],
        in_specs=[vmem] * 6,
        out_specs=[pl.BlockSpec(memory_space=pltpu.HBM), vmem, vmem],
        scratch_shapes=[
            pltpu.VMEM((SLOTS, TILE, COL_BLOCK), F32), pltpu.SemaphoreType.DMA((SLOTS,))
        ],
        compiler_params=pltpu.CompilerParams(vmem_limit_bytes=8 * 1024 * 1024),
        name="update",
    )(*(pltpu.with_memory_space_constraint(piece, pltpu.VMEM) for piece in pieces))


def on_device(trailing, panel_block):
    pieces = panel_call(trailing, panel_block)
    return tuple(update_call(*pieces))


def solution(mesh):
    in_specs = (P("row", "col"), P(("row", "col"), None))
    out_specs = (P("row", "col"), P(), P())
    return jax.shard_map(
        on_device, mesh=mesh, in_specs=in_specs, out_specs=out_specs, check_vma=False
    )
```

```python
import jax
import jax.numpy as jnp
from jax import lax
from jax.experimental import pallas as pl
from jax.experimental.pallas import tpu as pltpu
from jax.sharding import PartitionSpec as P

HIGHEST = lax.Precision.HIGHEST
MESH = pl.DeviceIdType.MESH
F32 = jnp.float32
BF16 = jnp.bfloat16

ROWS = 8
COLS = 16
SIDE = 4
NB = 128
SHARD = 160
HALF = 80
ROW_BLOCK = SHARD * COLS
COL_BLOCK = SHARD * ROWS
TILE = 256
STEP = 32
SLOTS = 3
WIDE = SIDE * SHARD


def dot(first, second, contract, precision=HIGHEST):
    return lax.dot_general(
        first, second, (contract, ((), ())), precision=precision, preferred_element_type=F32
    )


def split(value):
    high = value.astype(BF16)
    return high, (value - high.astype(F32)).astype(BF16)


def dot3(first, second, contract):
    (a, b), (c, d) = split(first), split(second)
    value = dot(a, c, contract, None)
    return value + (dot(a, d, contract, None) + dot(b, c, contract, None))


def factor(work, gram=None, bases=range(0, NB, STEP)):
    step = STEP
    down = lax.broadcasted_iota(jnp.int32, (NB, NB), 0)
    across = lax.broadcasted_iota(jnp.int32, (NB, NB), 1)
    if gram is not None:
        work[:, :NB] = gram
        work[:, NB:] = jnp.where(down == across, 1.0, 0.0)
    sub = lax.broadcasted_iota(jnp.int32, (step, 1), 0)
    for base in bases:
        rows = work[base : base + step, :]
        tall = [
            jnp.broadcast_to(rows[:, base + k : base + k + 1], (step, NB)) for k in range(step)
        ]
        for k in range(step):
            scale = lax.rsqrt(tall[k][k : k + 1, :])
            low = tall[k] * scale
            for m in range(k + 1, step):
                tall[m] = tall[m] - low * low[m : m + 1, :]
            top = rows[k : k + 1, :] * jnp.concatenate([scale, scale], axis=1)
            low = jnp.where(sub > k, low, 0.0)
            rows = jnp.where(sub == k, top, rows - jnp.concatenate([low, low], axis=1) * top)
        work[base : base + step, :] = rows
        if base + step < NB:
            change = dot(rows[:, :NB], rows, ((0,), (0,)))
            work[base + step :, :] = work[base + step :, :] - change[base + step :, :]
    if bases[-1] == NB - step:
        work[:, :NB] = jnp.where(across >= down, work[:, :NB], 0.0)
        work[:, NB:] = jnp.where(across <= down, work[:, NB:], 0.0)


class Exchange:
    def __init__(self, size, me, place, source, target, send_sem, recv_sem):
        self.size, self.me, self.place = size, me, place
        self.source, self.target = source, target
        self.send_sem, self.recv_sem = send_sem, recv_sem

    def each(self, action, unroll=False):
        def body(step, carry):
            action(lax.rem(self.me + step, self.size))
            return carry

        if unroll or self.size == SIDE:
            for step in range(1, self.size):
                body(step, 0)
        else:
            lax.fori_loop(1, self.size, body, 0)

    def copy(self, peer, slot):
        return pltpu.make_async_remote_copy(
            src_ref=self.source(peer),
            dst_ref=self.target(slot),
            send_sem=self.send_sem.at[peer],
            recv_sem=self.recv_sem.at[slot],
            device_id=self.place(peer),
            device_id_type=MESH,
        )

    def start(self):
        self.each(lambda peer: self.copy(peer, self.me).start(), unroll=True)

    def receive(self):
        self.each(lambda peer: self.copy(peer, peer).wait_recv(), unroll=True)

    def finish(self):
        self.each(lambda peer: self.copy(peer, peer).wait_send())


class Swap:
    def __init__(self, apart, place, source, target, there, here, send_sem, recv_sem):
        self.apart, self.here, self.source, self.target = apart, here, source, target
        self.copy = lambda slot: pltpu.make_async_remote_copy(
            src_ref=source, dst_ref=target(slot), send_sem=send_sem, recv_sem=recv_sem,
            device_id=place, device_id_type=MESH,
        )
        self.there = there

    def start(self):
        @pl.when(self.apart)
        def _():
            self.copy(self.there).start()

        @pl.when(jnp.logical_not(self.apart))
        def _():
            self.target(self.here)[...] = self.source[...]

    def receive(self):
        @pl.when(self.apart)
        def _():
            self.copy(self.here).wait_recv()

    def finish(self):
        @pl.when(self.apart)
        def _():
            self.copy(self.there).wait_send()


def eights(ref):
    return lambda index: ref.at[pl.ds(pl.multiple_of(index * 8, 8), 8), :]


def panel_kernel(
    trailing_hbm, panel_hbm,
    a_full, left_high, left_low, right, r_out, first_out,
    panel, x_high, x_low, mixed_t, a_high, a_low, p_rows, q_rows, q_wide, p_cols, q_cols,
    y_part, y_mate, y_half, y_ring, y_cols, y_rows,
    g_own, g_buf, g_part, g_all, h_own, h_buf, h_part, h_all, s_own, s_buf, s_part, s_all,
    work_one, work_two,
    a_sem, panel_sem, plane_send, plane_recv, axis_send, axis_recv, ring_send, ring_recv, one_send, one_recv,
):
    me_r, me_c = lax.axis_index("row"), lax.axis_index("col")
    z, core = me_r // 2, lax.rem(me_r, 2)
    y, x = me_c // SIDE, lax.rem(me_c, SIDE)
    in_plane = lambda peer: (me_r, peer)
    in_axis = lambda peer: (peer, me_c)
    in_x = lambda peer: (me_r, y * SIDE + peer)
    in_y = lambda peer: (me_r, peer * SIDE + x)
    in_z = lambda peer: (2 * peer + core, me_c)
    mate = (2 * z + 1 - core, me_c)
    out_r, out_c = lax.rem(me_c, ROWS), 2 * me_r + me_c // ROWS
    in_r, in_c = me_c // 2, ROWS * lax.rem(me_c, 2) + me_r
    apart = jnp.logical_not(jnp.logical_and(out_r == me_r, out_c == me_c))
    straight = core == x // 2
    turn_r = 2 * y + x // 2
    turn_x = jnp.where(straight, x, SIDE - 1 - x)
    turned = jnp.logical_not(jnp.logical_and(straight, y == z))

    fetch = pltpu.make_async_copy(panel_hbm, panel, panel_sem)
    fetch.start()
    load = pltpu.make_async_copy(trailing_hbm, a_full, a_sem)
    load.start()
    barrier = pltpu.get_barrier_semaphore()

    def signal(place):
        pl.semaphore_signal(barrier, inc=1, device_id=place, device_id_type=MESH)

    def greet(size, me, place):
        for step in range(1, size):
            signal(place(lax.rem(me + step, size)))

    greet(COLS, me_c, in_plane)
    greet(ROWS, me_r, in_axis)

    @pl.when(apart)
    def _():
        signal((out_r, out_c))
        signal((in_r, in_c))

    away = lambda half, j: jnp.logical_or(turned, j != (y, x)[half])
    for j in range(SIDE):

        @pl.when(away(0, j))
        def _():
            signal((2 * j + x // 2, z * SIDE + turn_x))

        @pl.when(away(1, j))
        def _():
            signal((2 * y + j // 2, z * SIDE + jnp.where(core == j // 2, j, SIDE - 1 - j)))

    fetch.wait()
    g_own[...] = dot(panel[...], panel[...], ((0,), (0,)))
    for half in range(2):
        p_rows[y, x, half] = panel[half * HALF : (half + 1) * HALF, :]
    pl.semaphore_wait(
        barrier, COLS + ROWS - 2 + jnp.where(apart, 2, 0) + jnp.where(turned, 8, 6)
    )

    def summed(own, buf, part, full, sem):
        scatter = Exchange(
            COLS, me_c, in_plane, eights(own), eights(buf),
            plane_send.at[sem], plane_recv.at[sem],
        )
        share = Exchange(
            ROWS, me_r, in_axis, lambda peer: eights(part)(me_r), eights(part),
            axis_send.at[sem], axis_recv.at[sem],
        )
        gather = Exchange(
            COLS, me_c, in_plane, lambda peer: eights(full)(me_c), eights(full),
            plane_send.at[sem + 3], plane_recv.at[sem + 3],
        )

        def total(source, count):
            value = source[:8, :]
            for k in range(1, count):
                value = value + source[k * 8 : k * 8 + 8, :]
            return value

        def one():
            eights(buf)(me_c)[...] = eights(own)(me_c)[...]
            scatter.start()

        def two():
            scatter.receive()
            eights(part)(me_r)[...] = total(buf, COLS)
            share.start()

        def three():
            share.receive()
            eights(full)(me_c)[...] = total(part, ROWS)
            gather.start()

        def finish():
            scatter.finish()
            share.finish()
            gather.finish()

        return one, two, three, gather.receive, finish

    def ring(place, me, source, target, sem):
        return Exchange(SIDE, me, place, source, target, ring_send.at[sem], ring_recv.at[sem])

    def plane_gather(rows, sem):
        first = (
            ring(in_y, y, lambda peer: rows.at[y, x, 0], lambda slot: rows.at[slot, x, 0], sem),
            ring(in_x, x, lambda peer: rows.at[y, x, 1], lambda slot: rows.at[y, slot, 1], sem + 1),
        )
        second = (
            ring(in_x, x, lambda peer: rows.at[:, x, 0], lambda slot: rows.at[:, slot, 0], sem + 2),
            ring(in_y, y, lambda peer: rows.at[y, :, 1], lambda slot: rows.at[slot, :, 1], sem + 3),
        )
        return first, second

    def start(pair):
        for item in pair:
            item.start()

    def receive(pair):
        for item in pair:
            item.receive()

    def axis_gather(cols, sem, mate_sem):
        along = ring(
            in_z, z, lambda peer: cols.at[z, core], lambda slot: cols.at[slot, core], sem
        )
        across = Swap(
            True, mate, cols.at[:, core], lambda slot: cols.at[:, slot], core, 1 - core,
            one_send.at[mate_sem], one_recv.at[mate_sem],
        )
        return along, across

    one, two, three, gram_all, gram_finish = summed(g_own, g_buf, g_part, g_all, 0)
    p_first, p_second = plane_gather(p_rows, 0)
    p_swap = Swap(
        apart, (out_r, out_c), panel, lambda slot: p_cols.at[slot // 2, lax.rem(slot, 2)],
        out_r, me_r, one_send.at[0], one_recv.at[0],
    )
    p_along, p_across = axis_gather(p_cols, 8, 1)
    start(p_first)
    one()
    two()
    p_swap.start()
    receive(p_first)
    start(p_second)
    three()
    load.wait()

    def split_rows(index, carry):
        rows = pl.ds(pl.multiple_of(index * 64, 64), 64)
        a_high[rows, :], a_low[rows, :] = split(a_full[rows, :])
        return carry

    lax.fori_loop(0, ROW_BLOCK // 64, split_rows, 0)
    gram_all()
    p_swap.receive()
    p_along.start()
    factor(work_one, g_all[...])
    first_out[...] = work_one[:, :NB]
    inverse = work_one[:, NB:]
    receive(p_second)

    def basis_rows(index, carry):
        rows = pl.ds(pl.multiple_of(index * WIDE, WIDE), WIDE)
        value = dot(p_rows[index].reshape(WIDE, NB), inverse, ((1,), (1,)))
        q_rows[rows, :] = value
        high, low = split(value.T)
        q_wide[:NB, rows] = high
        q_wide[NB:, rows] = low
        return carry

    lax.fori_loop(0, SIDE, basis_rows, 0)
    mine = q_rows[pl.ds(pl.multiple_of(me_c * SHARD, SHARD), SHARD), :]
    h_own[...] = dot(mine, mine, ((0,), (0,)))
    one, two, three, more_all, more_finish = summed(h_own, h_buf, h_part, h_all, 1)
    one()
    p_along.receive()
    p_across.start()

    piece = lambda place, k: pl.ds(pl.multiple_of((2 * place + k) * SHARD, SHARD), SHARD)
    y_pair = [
        pltpu.make_async_remote_copy(
            src_ref=y_part.at[piece(k, 1 - core), :], dst_ref=y_mate.at[k],
            send_sem=one_send.at[4 + k], recv_sem=one_recv.at[4 + k],
            device_id=mate, device_id_type=MESH,
        )
        for k in range(SIDE)
    ]

    def products(index, carry):
        cols = pl.ds(pl.multiple_of(index * TILE, TILE), TILE)
        wide = dot(q_wide[...], a_high[:, cols], ((1,), (0,)), None)
        value = wide[:NB, :] + wide[NB:, :]
        value = value + dot(q_wide[:NB, :], a_low[:, cols], ((1,), (0,)), None)
        y_part[cols, :] = value.T
        return carry

    for half, (begin, end) in enumerate(((0, 3), (3, 5))):
        lax.fori_loop(begin, end, products, 0)
        y_pair[2 * half].start()
        y_pair[2 * half + 1].start()
    two()

    def basis_cols(index, carry):
        rows = pl.ds(pl.multiple_of(index * 2 * SHARD, 2 * SHARD), 2 * SHARD)
        q_cols[rows, :] = dot(p_cols[index].reshape(2 * SHARD, NB), inverse, ((1,), (1,)))
        return carry

    p_across.receive()
    lax.fori_loop(0, SIDE, basis_cols, 0)
    s_own[...] = dot3(q_cols[...], y_part[...], ((0,), (0,)))
    center_one, center_two, center_three, center_all, center_finish = summed(
        s_own, s_buf, s_part, s_all, 2
    )
    center_one()
    for k in range(SIDE):
        y_pair[k].wait_recv()
        y_half[k] = y_part[piece(k, core), :] + y_mate[k]
    y_along = ring(in_z, z, lambda peer: y_half.at[peer], lambda slot: y_ring.at[slot], 9)
    y_along.start()
    three()
    center_two()
    y_ring[z] = y_half[z]
    gram_finish()
    for item in (*p_first, *p_second, p_swap, p_along):
        item.finish()
    y_along.receive()
    y_cols[z, core] = y_ring[0] + y_ring[1] + (y_ring[2] + y_ring[3])
    _, y_second = plane_gather(y_rows, 4)

    def y_copy(half, j, slot, recv):
        place = (turn_r, j * SIDE + turn_x) if half == 0 else (turn_r, z * SIDE + j)
        return pltpu.make_async_remote_copy(
            src_ref=y_cols.at[z, core, pl.ds(half * HALF, HALF)],
            dst_ref=y_rows.at[slot[0], slot[1], half],
            send_sem=ring_send.at[4 + half, j], recv_sem=ring_recv.at[4 + half, recv],
            device_id=place, device_id_type=MESH,
        )

    def y_each(action):
        for j in range(SIDE):
            for half in range(2):

                @pl.when(away(half, j))
                def _(half=half, j=j):
                    action(half, j)

    there = (z, turn_x)
    y_each(lambda half, j: y_copy(half, j, there, there[half]).start())

    @pl.when(jnp.logical_not(turned))
    def _():
        for half in range(2):
            y_rows[y, x, half] = y_cols[z, core, pl.ds(half * HALF, HALF)]

    y_columns, y_across = axis_gather(y_cols, 10, 8)
    y_columns.start()
    more_all()
    factor(work_two, h_all[...])
    center_three()
    second = work_two[:, NB:]
    gram_inverse = dot(second, second, ((0,), (0,)))

    def finish_x(index, carry):
        rows = pl.ds(pl.multiple_of(index * WIDE, WIDE), WIDE)
        x_high[rows, :], x_low[rows, :] = split(dot3(q_rows[rows, :], gram_inverse, ((1,), (0,))))
        return carry

    lax.fori_loop(0, SIDE, finish_x, 0)
    y_each(lambda half, j: y_copy(half, j, (j, x) if half == 0 else (y, j), j).wait_recv())
    start(y_second)
    y_columns.receive()
    y_across.start()
    center_all()
    center = 4.0 * s_all[...]
    y_across.receive()

    def finish_right(index, carry):
        rows = pl.ds(pl.multiple_of(index * WIDE, WIDE), WIDE)
        half = pl.ds(2 * index, 2)
        x_tile = dot3(q_cols[rows, :], gram_inverse, ((1,), (0,)))
        mixed = 2.0 * y_cols[half].reshape(WIDE, NB) - dot3(x_tile, center, ((1,), (0,)))
        for target, value in ((mixed_t, mixed), (right, 2.0 * x_tile)):
            high, low = split(value.T)
            target[:NB, rows] = high
            target[NB : 2 * NB, rows] = low
            target[2 * NB :, rows] = high
        return carry

    lax.fori_loop(0, 2, finish_right, 0)

    def update_x(index, carry):
        rows = pl.ds(pl.multiple_of(index * 2 * TILE, 2 * TILE), 2 * TILE)
        high = x_high[rows, :]
        wide = jnp.concatenate([high, high, x_low[rows, :]], axis=1)
        a_full[rows, :] = a_full[rows, :] - dot(wide, mixed_t[...], ((1,), (0,)), None)
        return carry

    lax.fori_loop(0, ROW_BLOCK // (2 * TILE), update_x, 0)
    r_out[...] = dot(work_two[:, :NB], work_one[:, :NB], ((1,), (0,)))
    more_finish()
    center_finish()
    for item in (p_across, y_along, y_columns):
        item.finish()
    for item in y_pair:
        item.wait_send()
    y_each(lambda half, j: y_copy(half, j, there, there[half]).wait_send())
    receive(y_second)

    def finish_y(index, carry):
        down, over = index // SIDE, lax.rem(index, SIDE)
        same = over // 2 == core
        source_x = jnp.where(same, over, SIDE - 1 - over)
        source_core = jnp.where(same, core, 1 - core)
        rank = lax.rem(source_x, 2) * ROWS + 2 * down + source_core
        rows = pl.ds(pl.multiple_of(rank * SHARD, SHARD), SHARD)
        left_high[rows, :], left_low[rows, :] = split(y_rows[down, over].reshape(SHARD, NB))
        return carry

    lax.fori_loop(0, COLS, finish_y, 0)

    for item in (*y_second, y_across):
        item.finish()


def panel_call(trailing, panel_block):
    vmem = pl.BlockSpec(memory_space=pltpu.VMEM)
    f32 = lambda *dims: pltpu.VMEM(dims, F32)
    bf16 = lambda *dims: pltpu.VMEM(dims, BF16)
    dma = lambda *dims: pltpu.SemaphoreType.DMA(dims)
    left, small = bf16(ROW_BLOCK, NB), f32(NB, NB)
    right = bf16(3 * NB, COL_BLOCK)
    plane = f32(SIDE, SIDE, 2, HALF, NB)
    axis = f32(SIDE, 2, SHARD, NB)
    ring = f32(SIDE, SHARD, NB)
    return pl.pallas_call(
        panel_kernel,
        out_shape=[f32(ROW_BLOCK, COL_BLOCK), left, left, right, small, small],
        in_specs=[pl.BlockSpec(memory_space=pl.ANY)] * 2,
        out_specs=[vmem] * 6,
        scratch_shapes=[
            f32(SHARD, NB), left, left, right,
            bf16(ROW_BLOCK, COL_BLOCK), bf16(ROW_BLOCK, COL_BLOCK),
            plane, f32(ROW_BLOCK, NB), bf16(2 * NB, ROW_BLOCK), axis, f32(COL_BLOCK, NB),
            f32(COL_BLOCK, NB), ring, ring, ring, axis, plane,
            *(3 * [small, small, f32(8 * ROWS, NB), small]),
            f32(NB, 2 * NB), f32(NB, 2 * NB),
            pltpu.SemaphoreType.DMA, pltpu.SemaphoreType.DMA, dma(6, COLS), dma(6, COLS), dma(3, ROWS), dma(3, ROWS),
            dma(11, SIDE), dma(11, SIDE), dma(9), dma(9),
        ],
        compiler_params=pltpu.CompilerParams(
            collective_id=0, has_side_effects=True, vmem_limit_bytes=36 * 1024 * 1024
        ),
        name="panel",
    )(trailing, pltpu.with_memory_space_constraint(panel_block, pltpu.HBM))


def update_kernel(
    trailing, left_high, left_low, right, r_in, first_in, out, r_out, first_out, ready, sems
):
    def send(index, slot):
        rows = pl.ds(pl.multiple_of(index * TILE, TILE), TILE)
        return pltpu.make_async_copy(ready.at[slot], out.at[rows, :], sems.at[slot])

    def body(index, carry):
        slot = lax.rem(index, SLOTS)

        @pl.when(index >= SLOTS)
        def _():
            send(index - SLOTS, slot).wait()

        rows = pl.ds(pl.multiple_of(index * TILE, TILE), TILE)
        high = left_high[rows, :]
        left = jnp.concatenate([high, high, left_low[rows, :]], axis=1)
        ready[slot] = trailing[rows, :] - dot(left, right[...], ((1,), (0,)), None)
        send(index, slot).start()
        return carry

    count = ROW_BLOCK // TILE
    lax.fori_loop(0, count, body, 0)
    r_out[...] = r_in[...]
    first_out[...] = first_in[...]
    for index in range(count - SLOTS, count):
        send(index, index % SLOTS).wait()


def update_call(*pieces):
    vmem = pl.BlockSpec(memory_space=pltpu.VMEM)
    small = jax.ShapeDtypeStruct((NB, NB), F32)
    return pl.pallas_call(
        update_kernel,
        out_shape=[jax.ShapeDtypeStruct((ROW_BLOCK, COL_BLOCK), F32), small, small],
        in_specs=[vmem] * 6,
        out_specs=[pl.BlockSpec(memory_space=pltpu.HBM), vmem, vmem],
        scratch_shapes=[
            pltpu.VMEM((SLOTS, TILE, COL_BLOCK), F32), pltpu.SemaphoreType.DMA((SLOTS,))
        ],
        compiler_params=pltpu.CompilerParams(vmem_limit_bytes=8 * 1024 * 1024),
        name="update",
    )(*(pltpu.with_memory_space_constraint(piece, pltpu.VMEM) for piece in pieces))


def on_device(trailing, panel_block):
    pieces = panel_call(trailing, panel_block)
    return tuple(update_call(*pieces))


def solution(mesh):
    in_specs = (P("row", "col"), P(("row", "col"), None))
    out_specs = (P("row", "col"), P(), P())
    return jax.shard_map(
        on_device, mesh=mesh, in_specs=in_specs, out_specs=out_specs, check_vma=False
    )
```

```python
import jax
import jax.numpy as jnp
from jax import lax
from jax.experimental import pallas as pl
from jax.experimental.pallas import tpu as pltpu
from jax.sharding import PartitionSpec as P

HIGHEST = lax.Precision.HIGHEST
MESH = pl.DeviceIdType.MESH
F32 = jnp.float32
BF16 = jnp.bfloat16

ROWS = 8
COLS = 16
SIDE = 4
NB = 128
SHARD = 160
HALF = 80
ROW_BLOCK = SHARD * COLS
COL_BLOCK = SHARD * ROWS
TILE = 256
STEP = 32
SLOTS = 2
LAST = 512
WIDE = SIDE * SHARD


def dot(first, second, contract, precision=HIGHEST):
    return lax.dot_general(
        first, second, (contract, ((), ())), precision=precision, preferred_element_type=F32
    )


def split(value):
    high = value.astype(BF16)
    return high, (value - high.astype(F32)).astype(BF16)


def dot3(first, second, contract):
    (a, b), (c, d) = split(first), split(second)
    value = dot(a, c, contract, None)
    return value + (dot(a, d, contract, None) + dot(b, c, contract, None))


def factor(work, gram=None, bases=range(0, NB, STEP)):
    step = STEP
    down = lax.broadcasted_iota(jnp.int32, (NB, NB), 0)
    across = lax.broadcasted_iota(jnp.int32, (NB, NB), 1)
    if gram is not None:
        work[:, :NB] = gram
        work[:, NB:] = jnp.where(down == across, 1.0, 0.0)
    sub = lax.broadcasted_iota(jnp.int32, (step, 1), 0)
    for base in bases:
        rows = work[base : base + step, :]
        tall = [
            jnp.broadcast_to(rows[:, base + k : base + k + 1], (step, NB)) for k in range(step)
        ]
        for k in range(step):
            scale = lax.rsqrt(tall[k][k : k + 1, :])
            low = tall[k] * scale
            for m in range(k + 1, step):
                tall[m] = tall[m] - low * low[m : m + 1, :]
            top = rows[k : k + 1, :] * jnp.concatenate([scale, scale], axis=1)
            low = jnp.where(sub > k, low, 0.0)
            rows = jnp.where(sub == k, top, rows - jnp.concatenate([low, low], axis=1) * top)
        work[base : base + step, :] = rows
        if base + step < NB:
            change = dot(rows[:, :NB], rows, ((0,), (0,)))
            work[base + step :, :] = work[base + step :, :] - change[base + step :, :]
    if bases[-1] == NB - step:
        work[:, :NB] = jnp.where(across >= down, work[:, :NB], 0.0)
        work[:, NB:] = jnp.where(across <= down, work[:, NB:], 0.0)


class Exchange:
    def __init__(self, size, me, place, source, target, send_sem, recv_sem):
        self.size, self.me, self.place = size, me, place
        self.source, self.target = source, target
        self.send_sem, self.recv_sem = send_sem, recv_sem

    def each(self, action, unroll=False):
        def body(step, carry):
            action(lax.rem(self.me + step, self.size))
            return carry

        if unroll or self.size == SIDE:
            for step in range(1, self.size):
                body(step, 0)
        else:
            lax.fori_loop(1, self.size, body, 0)

    def copy(self, peer, slot):
        return pltpu.make_async_remote_copy(
            src_ref=self.source(peer),
            dst_ref=self.target(slot),
            send_sem=self.send_sem.at[peer],
            recv_sem=self.recv_sem.at[slot],
            device_id=self.place(peer),
            device_id_type=MESH,
        )

    def start(self):
        self.each(lambda peer: self.copy(peer, self.me).start(), unroll=True)

    def receive(self):
        self.each(lambda peer: self.copy(peer, peer).wait_recv())

    def finish(self):
        self.each(lambda peer: self.copy(peer, peer).wait_send())


class Swap:
    def __init__(self, apart, place, source, target, there, here, send_sem, recv_sem):
        self.apart, self.here, self.source, self.target = apart, here, source, target
        self.copy = lambda slot: pltpu.make_async_remote_copy(
            src_ref=source, dst_ref=target(slot), send_sem=send_sem, recv_sem=recv_sem,
            device_id=place, device_id_type=MESH,
        )
        self.there = there

    def start(self):
        @pl.when(self.apart)
        def _():
            self.copy(self.there).start()

        @pl.when(jnp.logical_not(self.apart))
        def _():
            self.target(self.here)[...] = self.source[...]

    def receive(self):
        @pl.when(self.apart)
        def _():
            self.copy(self.here).wait_recv()

    def finish(self):
        @pl.when(self.apart)
        def _():
            self.copy(self.there).wait_send()


def eights(ref):
    return lambda index: ref.at[pl.ds(pl.multiple_of(index * 8, 8), 8), :]


def panel_kernel(
    trailing_hbm, panel_hbm,
    a_full, left_high, left_low, right, r_out, first_out,
    panel, x_high, x_low, mixed_t, a_high, a_low, p_rows, q_rows, q_wide, p_cols, q_cols,
    y_part, y_mate, y_half, y_ring, y_cols, y_rows,
    g_own, g_buf, g_part, g_all, h_own, h_buf, h_part, h_all, s_own, s_buf, s_part, s_all,
    work_one, work_two,
    a_sem, panel_sem, plane_send, plane_recv, axis_send, axis_recv, ring_send, ring_recv, one_send, one_recv,
):
    me_r, me_c = lax.axis_index("row"), lax.axis_index("col")
    z, core = me_r // 2, lax.rem(me_r, 2)
    y, x = me_c // SIDE, lax.rem(me_c, SIDE)
    in_plane = lambda peer: (me_r, peer)
    in_axis = lambda peer: (peer, me_c)
    in_x = lambda peer: (me_r, y * SIDE + peer)
    in_y = lambda peer: (me_r, peer * SIDE + x)
    in_z = lambda peer: (2 * peer + core, me_c)
    mate = (2 * z + 1 - core, me_c)
    out_r, out_c = lax.rem(me_c, ROWS), 2 * me_r + me_c // ROWS
    in_r, in_c = me_c // 2, ROWS * lax.rem(me_c, 2) + me_r
    apart = jnp.logical_not(jnp.logical_and(out_r == me_r, out_c == me_c))
    straight = core == x // 2
    turn_r = 2 * y + jnp.where(straight, core, 1 - core)
    turn_c = z * SIDE + jnp.where(straight, x, SIDE - 1 - x)
    turned = jnp.logical_not(jnp.logical_and(straight, y == z))

    fetch = pltpu.make_async_copy(panel_hbm, panel, panel_sem)
    fetch.start()
    load = pltpu.make_async_copy(trailing_hbm, a_full, a_sem)
    load.start()
    barrier = pltpu.get_barrier_semaphore()

    def signal(place):
        pl.semaphore_signal(barrier, inc=1, device_id=place, device_id_type=MESH)

    def greet(size, me, place):
        def body(step, carry):
            signal(place(lax.rem(me + step, size)))
            return carry

        lax.fori_loop(1, size, body, 0)

    greet(COLS, me_c, in_plane)
    greet(ROWS, me_r, in_axis)

    @pl.when(apart)
    def _():
        signal((out_r, out_c))
        signal((in_r, in_c))

    @pl.when(turned)
    def _():
        signal((turn_r, turn_c))

    fetch.wait()
    g_own[...] = dot(panel[...], panel[...], ((0,), (0,)))
    for half in range(2):
        p_rows[y, x, half] = panel[half * HALF : (half + 1) * HALF, :]
    pl.semaphore_wait(
        barrier, COLS + ROWS - 2 + jnp.where(apart, 2, 0) + jnp.where(turned, 1, 0)
    )

    def summed(own, buf, part, full, sem):
        scatter = Exchange(
            COLS, me_c, in_plane, eights(own), eights(buf),
            plane_send.at[sem], plane_recv.at[sem],
        )
        share = Exchange(
            ROWS, me_r, in_axis, lambda peer: eights(part)(me_r), eights(part),
            axis_send.at[sem], axis_recv.at[sem],
        )
        gather = Exchange(
            COLS, me_c, in_plane, lambda peer: eights(full)(me_c), eights(full),
            plane_send.at[sem + 3], plane_recv.at[sem + 3],
        )

        def total(source, count):
            value = source[:8, :]
            for k in range(1, count):
                value = value + source[k * 8 : k * 8 + 8, :]
            return value

        def one():
            eights(buf)(me_c)[...] = eights(own)(me_c)[...]
            scatter.start()

        def two():
            scatter.receive()
            eights(part)(me_r)[...] = total(buf, COLS)
            share.start()

        def three():
            share.receive()
            eights(full)(me_c)[...] = total(part, ROWS)
            gather.start()

        def finish():
            scatter.finish()
            share.finish()
            gather.finish()

        return one, two, three, gather.receive, finish

    def ring(place, me, source, target, sem):
        return Exchange(SIDE, me, place, source, target, ring_send.at[sem], ring_recv.at[sem])

    def plane_gather(rows, sem):
        first = (
            ring(in_y, y, lambda peer: rows.at[y, x, 0], lambda slot: rows.at[slot, x, 0], sem),
            ring(in_x, x, lambda peer: rows.at[y, x, 1], lambda slot: rows.at[y, slot, 1], sem + 1),
        )
        second = (
            ring(in_x, x, lambda peer: rows.at[:, x, 0], lambda slot: rows.at[:, slot, 0], sem + 2),
            ring(in_y, y, lambda peer: rows.at[y, :, 1], lambda slot: rows.at[slot, :, 1], sem + 3),
        )
        return first, second

    def start(pair):
        for item in pair:
            item.start()

    def receive(pair):
        for item in pair:
            item.receive()

    def axis_gather(cols, sem, mate_sem):
        along = ring(
            in_z, z, lambda peer: cols.at[z, core], lambda slot: cols.at[slot, core], sem
        )
        across = Swap(
            True, mate, cols.at[:, core], lambda slot: cols.at[:, slot], core, 1 - core,
            one_send.at[mate_sem], one_recv.at[mate_sem],
        )
        return along, across

    one, two, three, gram_all, gram_finish = summed(g_own, g_buf, g_part, g_all, 0)
    p_first, p_second = plane_gather(p_rows, 0)
    p_swap = Swap(
        apart, (out_r, out_c), panel, lambda slot: p_cols.at[slot // 2, lax.rem(slot, 2)],
        out_r, me_r, one_send.at[0], one_recv.at[0],
    )
    p_along, p_across = axis_gather(p_cols, 8, 1)
    one()
    start(p_first)
    two()
    p_swap.start()
    receive(p_first)
    start(p_second)
    three()
    load.wait()

    def split_rows(index, carry):
        rows = pl.ds(pl.multiple_of(index * 64, 64), 64)
        a_high[rows, :], a_low[rows, :] = split(a_full[rows, :])
        return carry

    lax.fori_loop(0, ROW_BLOCK // 64, split_rows, 0)
    gram_all()
    p_swap.receive()
    p_along.start()
    factor(work_one, g_all[...])
    first_out[...] = work_one[:, :NB]
    inverse = work_one[:, NB:]
    receive(p_second)

    def basis_rows(index, carry):
        rows = pl.ds(pl.multiple_of(index * WIDE, WIDE), WIDE)
        value = dot(p_rows[index].reshape(WIDE, NB), inverse, ((1,), (1,)))
        q_rows[rows, :] = value
        high, low = split(value.T)
        q_wide[:NB, rows] = high
        q_wide[NB:, rows] = low
        return carry

    lax.fori_loop(0, SIDE, basis_rows, 0)
    mine = q_rows[pl.ds(pl.multiple_of(me_c * SHARD, SHARD), SHARD), :]
    h_own[...] = dot(mine, mine, ((0,), (0,)))
    one, two, three, more_all, more_finish = summed(h_own, h_buf, h_part, h_all, 1)
    one()
    p_along.receive()
    p_across.start()

    piece = lambda place, k: pl.ds(pl.multiple_of((2 * place + k) * SHARD, SHARD), SHARD)
    y_pair = [
        pltpu.make_async_remote_copy(
            src_ref=y_part.at[piece(k, 1 - core), :], dst_ref=y_mate.at[k],
            send_sem=one_send.at[4 + k], recv_sem=one_recv.at[4 + k],
            device_id=mate, device_id_type=MESH,
        )
        for k in range(SIDE)
    ]

    def products(index, carry):
        cols = pl.ds(pl.multiple_of(index * TILE, TILE), TILE)
        wide = dot(q_wide[...], a_high[:, cols], ((1,), (0,)), None)
        value = wide[:NB, :] + wide[NB:, :]
        value = value + dot(q_wide[:NB, :], a_low[:, cols], ((1,), (0,)), None)
        y_part[cols, :] = value.T
        return carry

    for half, (begin, end) in enumerate(((0, 3), (3, 5))):
        lax.fori_loop(begin, end, products, 0)
        y_pair[2 * half].start()
        y_pair[2 * half + 1].start()
    two()

    def basis_cols(index, carry):
        rows = pl.ds(pl.multiple_of(index * 2 * SHARD, 2 * SHARD), 2 * SHARD)
        q_cols[rows, :] = dot(p_cols[index].reshape(2 * SHARD, NB), inverse, ((1,), (1,)))
        return carry

    p_across.receive()
    lax.fori_loop(0, SIDE, basis_cols, 0)
    s_own[...] = dot3(q_cols[...], y_part[...], ((0,), (0,)))
    center_one, center_two, center_three, center_all, center_finish = summed(
        s_own, s_buf, s_part, s_all, 2
    )
    center_one()
    for k in range(SIDE):
        y_pair[k].wait_recv()
        y_half[k] = y_part[piece(k, core), :] + y_mate[k]
    y_along = ring(in_z, z, lambda peer: y_half.at[peer], lambda slot: y_ring.at[slot], 9)
    y_along.start()
    three()
    y_ring[z] = y_half[z]
    gram_finish()
    for item in (*p_first, *p_second, p_swap, p_along):
        item.finish()
    y_along.receive()
    y_cols[z, core] = y_ring[0] + y_ring[1] + (y_ring[2] + y_ring[3])
    y_first, y_second = plane_gather(y_rows, 4)
    y_swaps = [
        Swap(
            turned, (turn_r, turn_c), y_cols.at[z, core, pl.ds(half * HALF, HALF)],
            lambda slot, half=half: y_rows.at[slot // SIDE, lax.rem(slot, SIDE), half],
            turn_c, me_c, one_send.at[2 + half], one_recv.at[2 + half],
        )
        for half in range(2)
    ]
    y_columns, y_across = axis_gather(y_cols, 10, 8)
    start(y_swaps)
    y_columns.start()
    center_two()
    more_all()
    factor(work_two, h_all[...])
    receive(y_swaps)
    start(y_first)
    center_three()
    r_out[...] = dot(work_two[:, :NB], work_one[:, :NB], ((1,), (0,)))
    second = work_two[:, NB:]
    gram_inverse = dot(second, second, ((0,), (0,)))

    def finish_x(index, carry):
        rows = pl.ds(pl.multiple_of(index * WIDE, WIDE), WIDE)
        x_high[rows, :], x_low[rows, :] = split(dot3(q_rows[rows, :], gram_inverse, ((1,), (0,))))
        return carry

    lax.fori_loop(0, SIDE, finish_x, 0)
    receive(y_first)
    start(y_second)
    y_columns.receive()
    y_across.start()
    center_all()
    center = 4.0 * s_all[...]
    y_across.receive()

    def finish_right(index, carry):
        rows = pl.ds(pl.multiple_of(index * WIDE, WIDE), WIDE)
        half = pl.ds(2 * index, 2)
        x_tile = dot3(q_cols[rows, :], gram_inverse, ((1,), (0,)))
        mixed = 2.0 * y_cols[half].reshape(WIDE, NB) - dot3(x_tile, center, ((1,), (0,)))
        for target, value in ((mixed_t, mixed), (right, 2.0 * x_tile)):
            high, low = split(value.T)
            target[:NB, rows] = high
            target[NB : 2 * NB, rows] = low
            target[2 * NB :, rows] = high
        return carry

    lax.fori_loop(0, 2, finish_right, 0)

    def update_x(index, carry):
        rows = pl.ds(pl.multiple_of(index * TILE, TILE), TILE)
        high = x_high[rows, :]
        wide = jnp.concatenate([high, high, x_low[rows, :]], axis=1)
        a_full[rows, :] = a_full[rows, :] - dot(wide, mixed_t[...], ((1,), (0,)), None)
        return carry

    lax.fori_loop(0, ROW_BLOCK // TILE, update_x, 0)
    more_finish()
    center_finish()
    for item in (p_across, y_along, *y_swaps, *y_first, y_columns):
        item.finish()
    for item in y_pair:
        item.wait_send()
    receive(y_second)

    def finish_y(index, carry):
        down, over = index // SIDE, lax.rem(index, SIDE)
        same = over // 2 == core
        source_x = jnp.where(same, over, SIDE - 1 - over)
        source_core = jnp.where(same, core, 1 - core)
        rank = lax.rem(source_x, 2) * ROWS + 2 * down + source_core
        rows = pl.ds(pl.multiple_of(rank * SHARD, SHARD), SHARD)
        left_high[rows, :], left_low[rows, :] = split(y_rows[down, over].reshape(SHARD, NB))
        return carry

    lax.fori_loop(0, COLS, finish_y, 0)

    for item in (*y_second, y_across):
        item.finish()


def panel_call(trailing, panel_block):
    vmem = pl.BlockSpec(memory_space=pltpu.VMEM)
    f32 = lambda *dims: pltpu.VMEM(dims, F32)
    bf16 = lambda *dims: pltpu.VMEM(dims, BF16)
    dma = lambda *dims: pltpu.SemaphoreType.DMA(dims)
    left, small = bf16(ROW_BLOCK, NB), f32(NB, NB)
    right = bf16(3 * NB, COL_BLOCK)
    plane = f32(SIDE, SIDE, 2, HALF, NB)
    axis = f32(SIDE, 2, SHARD, NB)
    ring = f32(SIDE, SHARD, NB)
    return pl.pallas_call(
        panel_kernel,
        out_shape=[f32(ROW_BLOCK, COL_BLOCK), left, left, right, small, small],
        in_specs=[pl.BlockSpec(memory_space=pl.ANY)] * 2,
        out_specs=[vmem] * 6,
        scratch_shapes=[
            f32(SHARD, NB), left, left, right,
            bf16(ROW_BLOCK, COL_BLOCK), bf16(ROW_BLOCK, COL_BLOCK),
            plane, f32(ROW_BLOCK, NB), bf16(2 * NB, ROW_BLOCK), axis, f32(COL_BLOCK, NB),
            f32(COL_BLOCK, NB), ring, ring, ring, axis, plane,
            *(3 * [small, small, f32(8 * ROWS, NB), small]),
            f32(NB, 2 * NB), f32(NB, 2 * NB),
            pltpu.SemaphoreType.DMA, pltpu.SemaphoreType.DMA, dma(6, COLS), dma(6, COLS), dma(3, ROWS), dma(3, ROWS),
            dma(11, SIDE), dma(11, SIDE), dma(9), dma(9),
        ],
        compiler_params=pltpu.CompilerParams(
            collective_id=0, has_side_effects=True, vmem_limit_bytes=36 * 1024 * 1024
        ),
        name="panel",
    )(trailing, pltpu.with_memory_space_constraint(panel_block, pltpu.HBM))


def update_kernel(
    trailing, left_high, left_low, right, r_in, first_in, out, r_out, first_out, ready, sems
):
    def send(index, slot):
        rows = pl.ds(pl.multiple_of(index * LAST, LAST), LAST)
        return pltpu.make_async_copy(ready.at[slot], out.at[rows, :], sems.at[slot])

    def body(index, carry):
        slot = lax.rem(index, SLOTS)

        @pl.when(index >= SLOTS)
        def _():
            send(index - SLOTS, slot).wait()

        rows = pl.ds(pl.multiple_of(index * LAST, LAST), LAST)
        high = left_high[rows, :]
        left = jnp.concatenate([high, high, left_low[rows, :]], axis=1)
        ready[slot] = trailing[rows, :] - dot(left, right[...], ((1,), (0,)), None)
        send(index, slot).start()
        return carry

    count = ROW_BLOCK // LAST
    lax.fori_loop(0, count, body, 0)
    r_out[...] = r_in[...]
    first_out[...] = first_in[...]
    for index in range(count - SLOTS, count):
        send(index, index % SLOTS).wait()


def update_call(*pieces):
    vmem = pl.BlockSpec(memory_space=pltpu.VMEM)
    small = jax.ShapeDtypeStruct((NB, NB), F32)
    return pl.pallas_call(
        update_kernel,
        out_shape=[jax.ShapeDtypeStruct((ROW_BLOCK, COL_BLOCK), F32), small, small],
        in_specs=[vmem] * 6,
        out_specs=[pl.BlockSpec(memory_space=pltpu.HBM), vmem, vmem],
        scratch_shapes=[
            pltpu.VMEM((SLOTS, LAST, COL_BLOCK), F32), pltpu.SemaphoreType.DMA((SLOTS,))
        ],
        compiler_params=pltpu.CompilerParams(vmem_limit_bytes=12 * 1024 * 1024),
        name="update",
    )(*(pltpu.with_memory_space_constraint(piece, pltpu.VMEM) for piece in pieces))


def on_device(trailing, panel_block):
    pieces = panel_call(trailing, panel_block)
    return tuple(update_call(*pieces))


def solution(mesh):
    in_specs = (P("row", "col"), P(("row", "col"), None))
    out_specs = (P("row", "col"), P(), P())
    return jax.shard_map(
        on_device, mesh=mesh, in_specs=in_specs, out_specs=out_specs, check_vma=False
    )
```
